256 devices in a mesh: ray: 32 (over x, y, core), tile: 8 (over z).
Axes of the slice: x: 4, y: 4, z: 8, core: 2. Of those that a mesh axis runs over, the one named last changes fastest.
Arguments:
- data: float32 [262144], P(('ray', 'tile')), may hold values from -6 to 6
- blocks: bfloat16 [32, 8, 128, 128, 128], P('ray', 'tile'), may hold values from -0.1875 to 0.1875
- block_cols: int32 [32, 8, 128], P('ray', 'tile'), may hold values from 0 to 1023, as said below
- block_rows: int32 [32, 8, 128], P('ray', 'tile'), may hold values from 0 to 63
- block_counts: int32 [32, 8], P('ray', 'tile'), may hold values from 1 to 128, as said below
- reg_weight: float32 [32, 256, 128], P('tile', 'ray'), may hold values from 0.05 to 0.5
Outputs:
- model: float32 [32, 256, 128], P('tile', 'ray')
- ray_vector: float32 [262144], P(('ray', 'tile'))
The draws below stay inside these ranges and needn't reach their ends.
Inputs may be any that keep to these rules, and one draw needn't show every extreme that they name: `block_counts`: some ray group has exactly 128 live blocks in some tile in every draw. `block_cols`: column c of a tile lies in the cells of ray index (c % 256) // 8. Of the 128 slots of one ray group in one tile, live or not, at most 8 name columns of one ray index, and in every draw 128 // 8 ray indices are named by exactly 8 slots.
All inputs are finite; a program needn't handle non-finite values.
Results may differ from the reference program's by a relative error of at most 0.0043.
Values may be sent and summed in bfloat16 or wider, within the bound.
No kernel may reach another device: no remote copies, remote signals or barrier semaphores. Data moves between devices by JAX's collectives and lax.ppermute only.
A program may use at most 64 MiB of HBM per device.

```python
import math
import jax
import jax.numpy as jnp
from jax import lax

CZ = 128
RB = 128
CX = 4
CY = 8
NB = 128
ROWBLK = 64
ITERS = 2
NX = 32
NY = 256
RAYS = 262144
CAP = 8
N_RAY = 32
N_TILE = 8


def draw_block_counts(key, part):
    key = jax.random.fold_in(key, 7)
    first, second, third, fourth = jax.random.split(key, 4)
    level = jax.random.randint(first, (N_RAY, 1), 0, 4)
    jitter = jax.random.randint(second, (N_RAY, N_TILE), 0, NB // 16 + 1)
    counts = jnp.maximum(1, NB * 2 ** level // 8 - jitter)
    pick_ray = jax.random.randint(third, (), 0, N_RAY)
    pick_tile = jax.random.randint(fourth, (), 0, N_TILE)
    chosen = (jnp.arange(N_RAY)[:, None] == pick_ray) & (jnp.arange(N_TILE)[None, :] == pick_tile)
    return jnp.where(chosen, NB, counts).astype(jnp.int32)


def draw_block_cols(key, part):
    key = jax.random.fold_in(key, 11)
    first, second, third, fourth = jax.random.split(key, 4)
    many = N_RAY * N_TILE
    keys = jax.random.split(first, many)
    orders = jax.vmap(lambda one: jax.random.permutation(one, NB))(keys)
    offset = jax.random.randint(second, (many, 1), 0, N_RAY)
    owner = (orders // CAP + offset) % N_RAY
    across = jax.random.randint(third, (many, NB), 0, CX)
    within = jax.random.randint(fourth, (many, NB), 0, CY)
    columns = across * (CY * N_RAY) + owner * CY + within
    return columns.reshape(N_RAY, N_TILE, NB).astype(jnp.int32)


def plant(drawn, stream_key, smallest, top_value):
    longest = drawn.shape.index(max(drawn.shape))
    spots = []
    for shift in (0, 1):
        where = [jax.random.randint(jax.random.fold_in(stream_key, axis), (), 0, length) for axis, length in enumerate(drawn.shape)]
        where[longest] = (where[longest] + shift) % drawn.shape[longest]
        spots.append(tuple(where))
    return drawn.at[spots[0]].set(smallest).at[spots[1]].set(top_value)


def block_levels(own_key, shape, cuts, least, high):
    loudness = 1.0
    for dim, shards_of in cuts:
        steps = jax.random.uniform(jax.random.fold_in(jax.random.fold_in(own_key, 6), dim), (shards_of,), jnp.float32, least / len(cuts), high / len(cuts))
        loudness = loudness * jnp.repeat(jnp.exp(steps), shape[dim] // shards_of).reshape((-1,) + (1,) * (len(shape) - 1 - dim))
    return loudness


def gaussian(rng, extent, width, bound, cuts=(), kind=jnp.bfloat16):
    values = jax.random.normal(rng, extent, jnp.float32) * width
    if len(cuts) > 0:
        values = block_levels(rng, extent, cuts, -0.22, 0.18) * values
    return jnp.clip(values, min=-bound, max=bound).astype(kind)


def setup_inputs(seed: int = 0) -> dict:
    arg_keys = jax.random.split(jax.random.key(seed), 7)
    data = gaussian(arg_keys[0], (RAYS,), 1.0, 6.0, ((0, 256),), jnp.float32)
    blocks = gaussian(arg_keys[1], (N_RAY, N_TILE, NB, RB, CZ), 0.03125, 0.1875, ((0, 32), (1, 8)))
    block_cols = draw_block_cols(jax.random.fold_in(arg_keys[6], 71), 0)
    block_rows = plant(jax.random.randint(arg_keys[3], (N_RAY, N_TILE, NB), 0, ROWBLK), jax.random.fold_in(arg_keys[3], 1), 0, ROWBLK - 1).astype(jnp.int32)
    block_counts = draw_block_counts(jax.random.fold_in(arg_keys[6], 71), 0)
    reg_weight = jnp.clip(jnp.exp(math.log(0.5) - 2.3025851 * jax.random.uniform(arg_keys[5], (NX, NY, CZ), jnp.float32) ** block_levels(arg_keys[5], (NX, NY, CZ), ((0, 8), (1, 32)), -0.2, 0.2)), 0.05, 0.5)
    return dict(data=data, blocks=blocks, block_cols=block_cols, block_rows=block_rows, block_counts=block_counts, reg_weight=reg_weight)


eps = 1e-06

def laplace(field):
    padded = jnp.pad(field, 1)
    beside = padded[2:, 1:-1, 1:-1] + padded[:-2, 1:-1, 1:-1]
    beside = beside + padded[1:-1, 2:, 1:-1] + padded[1:-1, :-2, 1:-1]
    beside = beside + padded[1:-1, 1:-1, 2:] + padded[1:-1, 1:-1, :-2]
    return 6.0 * field - beside

def reference(data, blocks, block_cols, block_rows, block_counts, reg_weight):
    grid_y = CY * N_RAY
    tile_cols = CX * grid_y
    tiles = jnp.arange(N_TILE).astype(jnp.int32)[:, None]
    live = jnp.arange(NB).astype(jnp.int32)[None, None, :] < block_counts[:, :, None]
    flat_cols = (tiles[None, :, :] * tile_cols + block_cols).astype(jnp.int32)

    def forward(field):
        tiled = field.astype(jnp.bfloat16).reshape(N_TILE, tile_cols, CZ)

        def group(args):
            values, cols, rows, mask = args
            segment = tiled[tiles, cols].astype(jnp.float32)
            product = jnp.einsum('tbrc,tbc->tbr', values.astype(jnp.float32), segment)
            product = jnp.where(mask[:, :, None], product, 0.0)
            return jax.ops.segment_sum(product.reshape(-1, RB), rows.reshape(-1), num_segments=ROWBLK).reshape(-1)
        return lax.map(group, (blocks, block_cols, block_rows, live)).reshape(-1)

    def transpose(rays_half):
        grouped = rays_half.reshape(N_RAY, ROWBLK, RB)

        def add(total, args):
            values, rows, index, mask, vector = args
            picked = vector[rows].astype(jnp.float32)
            contrib = jnp.einsum('tbrc,tbr->tbc', values.astype(jnp.float32), picked)
            contrib = jnp.where(mask[:, :, None], contrib, 0.0)
            return (total + jax.ops.segment_sum(contrib.reshape(-1, CZ), index.reshape(-1), num_segments=N_TILE * tile_cols), None)
        total, _ = lax.scan(add, jnp.zeros((N_TILE * tile_cols, CZ), jnp.float32), (blocks, block_rows, flat_cols, live, grouped))
        return total.reshape(N_TILE * CX, grid_y, CZ)
    raw_rays = data
    raw_cells = jnp.zeros_like(reg_weight)
    v_prev = jnp.zeros_like(reg_weight)
    u_rays = data
    u_cells = raw_cells
    alpha_prev = jnp.float32(0.0)
    for section in range(ITERS + 1):
        if section > 0:
            raw_rays = forward(v_prev) - alpha_prev * u_rays
            raw_cells = reg_weight * laplace(v_prev) - alpha_prev * u_cells
        beta = jnp.sqrt(jnp.sum(raw_rays * raw_rays) + jnp.sum(raw_cells * raw_cells) + eps)
        z_field = transpose(raw_rays.astype(jnp.bfloat16)) + laplace(reg_weight * raw_cells)
        v_raw = z_field / beta - beta * v_prev
        alpha = jnp.sqrt(jnp.sum(v_raw * v_raw) + eps)
        u_rays = raw_rays / beta
        u_cells = raw_cells / beta
        v_now = v_raw / alpha
        if section == 0:
            w_dir = v_now
            phibar = beta
            rhobar = alpha
            model = jnp.zeros_like(reg_weight)
        else:
            rho = jnp.sqrt(rhobar * rhobar + beta * beta)
            cosine = rhobar / rho
            sine = beta / rho
            theta = sine * alpha
            rhobar = -cosine * alpha
            phi = cosine * phibar
            phibar = sine * phibar
            model = model + phi / rho * w_dir
            w_dir = v_now - theta / rho * w_dir
        v_prev = v_now
        alpha_prev = alpha
    return (model, u_rays)
```

```python
import jax
import jax.numpy as jnp
from jax import lax
from jax.experimental import pallas as pl
from jax.experimental.pallas import tpu as pltpu
from jax.sharding import PartitionSpec as P

RAY = 32
TILE = 8
CAP = 8
CX = 4
CY = 8
CELLS = CX * CY
SLOTS = 128
LANES = 128
KB = 64
KOWN = KB // TILE
MSG = 2 * CAP
TMSG = KB + CELLS + 16
eps = 1e-06

F32 = jnp.float32
BF16 = jnp.bfloat16


def iota(shape, dim):
    return lax.broadcasted_iota(jnp.int32, shape, dim)


def dot(a, b, ca, cb):
    return lax.dot_general(a, b, (((ca,), (cb,)), ((), ())), preferred_element_type=F32)


def onehot_dot(hot, x, ca, cb):
    high = x.astype(BF16)
    rest = x - high.astype(F32)
    mid = rest.astype(BF16)
    low = (rest - mid.astype(F32)).astype(BF16)
    return dot(hot, high, ca, cb) + (dot(hot, mid, ca, cb) + dot(hot, low, ca, cb))


def total(x):
    return jnp.sum(jnp.sum(x, axis=0, keepdims=True), axis=1, keepdims=True)


def wide(x):
    return jnp.broadcast_to(x, (1, LANES))


def lane_sides(f):
    lane = iota(f.shape, 1)
    left = jnp.where(lane == 0, 0.0, pltpu.roll(f, 1, 1))
    right = jnp.where(lane == LANES - 1, 0.0, pltpu.roll(f, LANES - 1, 1))
    return left + right


def row_sides(f, low, high):
    row = iota(f.shape, 0)
    below = jnp.where(row == 0, low, pltpu.roll(f, 1, 0))
    above = jnp.where(row == CY - 1, high, pltpu.roll(f, CY - 1, 0))
    return below + above


def products_t(rays, blocks, r_hot):
    picked = dot(r_hot, rays.astype(BF16), 0, 0)
    row = iota((8, LANES), 0)
    out = []
    for q in range(SLOTS // 8):
        p = picked[8 * q : 8 * q + 8, :]
        lhs = jnp.concatenate([jnp.where(row == i, p, 0.0) for i in range(8)], axis=1)
        out.append(dot(lhs.astype(BF16), blocks[8 * q : 8 * q + 8].reshape(8 * LANES, LANES), 1, 0))
    return jnp.concatenate(out, axis=0)


def products(x_t, blocks, r_hot):
    lane = iota((LANES, SLOTS), 1)
    half = SLOTS // 2
    rhs = jnp.concatenate(
        [jnp.where(lane < half, x_t, 0.0), jnp.where(lane >= half, x_t, 0.0)], axis=0
    ).astype(BF16)
    acc = jnp.zeros((LANES, SLOTS), F32)
    for b in range(half):
        res = dot(jnp.concatenate([blocks[b], blocks[b + half]], axis=1), rhs, 1, 0)
        acc = jnp.where((lane == b) | (lane == b + half), res, acc)
    return onehot_dot(r_hot, acc, 1, 1)


def send_edges(send, tile8, scratch, rows_low, rows_high, scalar, ray):
    for x in range(CX):
        scratch[0, x : x + 1, :] = rows_low[x]
        scratch[1, x : x + 1, :] = rows_high[x]
    filler = jnp.broadcast_to(scalar, (8 - CX, LANES))
    scratch[0, CX:8, :] = filler
    scratch[1, CX:8, :] = filler
    low, high = scratch[0], scratch[1]
    for d in range(RAY):
        send[d, CAP:MSG, :] = jnp.where(d > ray, high, low)


def kernel_start(pos_ref, recv, cols, rows, count, blocks, send, p_out, r_out):
    col = cols[...]
    live = iota((1, SLOTS), 1) < count[0, 0]
    slab = RAY * CY
    owner = lax.div(lax.rem(col, slab), CY)
    local = lax.div(col, slab) * CY + lax.rem(col, CY)
    own_hot = iota((RAY, SLOTS), 0) == owner
    before = (iota((SLOTS, SLOTS), 0) < iota((SLOTS, SLOTS), 1)).astype(F32).astype(BF16)
    earlier = dot(own_hot.astype(F32).astype(BF16), before, 1, 0)
    rank = jnp.sum(jnp.where(own_hot, earlier, 0.0), axis=0, keepdims=True).astype(jnp.int32)
    p_bool = (iota((RAY * CAP, SLOTS), 0) == owner * CAP + rank) & live
    p_f = p_bool.astype(F32)
    p_hot = p_f.astype(BF16)
    r_hot = ((iota((KB, SLOTS), 0) == rows[...]) & live).astype(F32).astype(BF16)
    p_out[...] = p_hot
    r_out[...] = r_hot
    data = recv[:, 0:KOWN, :].reshape(KB, LANES)
    contrib = products_t(data, blocks, r_hot)
    send[:, 0:CAP, :] = onehot_dot(p_hot, contrib, 1, 0).reshape(RAY, CAP, LANES)
    ids = jnp.sum(p_f * (local + 1).astype(F32), axis=1, keepdims=True) - 1.0
    lane = iota((RAY * CAP, LANES), 1)
    note = jnp.where(lane < LANES // 2, ids, total(data * data))
    send[:, CAP:MSG, :] = note.reshape(RAY, CAP, LANES)


def spread(send, q_hot, v_raw):
    send[:, 0:CAP, :] = onehot_dot(q_hot, v_raw, 1, 0).reshape(RAY, CAP, LANES)


def kernel_first_v(pos_ref, recv, send, v_out, q_out, beta_out, scratch):
    contrib = recv[:, 0:CAP, :].reshape(RAY * CAP, LANES)
    note = recv[:, CAP:MSG, :].reshape(RAY * CAP, LANES)
    lane = iota((RAY * CAP, LANES), 1)
    row = iota((RAY * CAP, LANES), 0)
    q_hot = ((note == lane.astype(F32)) & (lane < CELLS)).astype(F32).astype(BF16)
    q_out[...] = q_hot
    squares = total(jnp.where((lane == LANES - 1) & (lax.rem(row, CAP) == 0), note, 0.0))
    beta = jnp.sqrt(squares + eps)
    beta_out[...] = wide(beta)
    v_raw = onehot_dot(q_hot, contrib, 0, 0) / beta
    v_out[...] = v_raw[0:CELLS]
    spread(send, q_hot, v_raw)
    low = [v_raw[CY * x : CY * x + 1, :] for x in range(CX)]
    high = [v_raw[CY * x + CY - 1 : CY * x + CY, :] for x in range(CX)]
    send_edges(send, None, scratch, low, high, total(v_raw * v_raw), pos_ref[0])


def kernel_forward(pos_ref, recv, p_hot, r_hot, blocks, v_raw, send):
    ray = pos_ref[0]
    values = recv[:, 0:CAP, :].reshape(RAY * CAP, LANES).astype(BF16)
    x_t = dot(values, p_hot[...], 0, 0)
    part = products(x_t, blocks, r_hot[...])
    norm = jnp.zeros((8, LANES), F32)
    for d in range(RAY):
        norm = norm + recv[d, CAP:MSG, :]
    row = iota((8, LANES), 0)
    low = jnp.where(ray > 0, recv[jnp.maximum(ray - 1, 0), CAP:MSG, :], 0.0)
    high = jnp.where(ray < RAY - 1, recv[jnp.minimum(ray + 1, RAY - 1), CAP:MSG, :], 0.0)
    low = jnp.where(row < CX, low, norm)
    high = jnp.where(row < CX, high, norm)
    mine = v_raw[...]
    for t in range(TILE):
        send[t, 0:KB, :] = part
        send[t, KB : KB + CELLS, :] = mine
        send[t, KB + CELLS : KB + CELLS + 8, :] = low
        send[t, KB + CELLS + 8 : TMSG, :] = high


def gathered(recv):
    kv = recv[0, 0:KB, :]
    norm = recv[0, TMSG - 1 : TMSG, :]
    for t in range(1, TILE):
        kv = kv + recv[t, 0:KB, :]
        norm = norm + recv[t, TMSG - 1 : TMSG, :]
    return kv, jnp.sqrt(norm + eps)


def slab_laplace(recv, index):
    t, x = divmod(index, CX)

    def cells(i):
        t, x = divmod(i, CX)
        start = KB + CY * x
        return recv[t, start : start + CY, :]

    f = cells(index)
    base = KB + CELLS + x
    beside = row_sides(f, recv[t, base : base + 1, :], recv[t, base + 8 : base + 9, :])
    beside = beside + lane_sides(f)
    if index > 0:
        beside = beside + cells(index - 1)
    if index < TILE * CX - 1:
        beside = beside + cells(index + 1)
    return 6.0 * f - beside


def kernel_back(
    pos_ref, recv, start, beta0, blocks, p_hot, r_hot, send, raw1_out, raw2_out, alpha_out, nq_out, scratch, field
):
    ray, tile = pos_ref[0], pos_ref[1]
    kv, alpha = gathered(recv)
    alpha_out[...] = alpha
    data = start[:, 0:KOWN, :].reshape(KB, LANES)
    raw1 = kv / alpha - alpha * (data / beta0[...])
    raw1_out[...] = raw1
    field[0] = jnp.zeros((CY, LANES), F32)
    field[TILE * CX + 1] = jnp.zeros((CY, LANES), F32)
    squares = jnp.zeros((CY, LANES), F32)
    for i in range(TILE * CX):
        t, x = divmod(i, CX)
        weight = start[t, KOWN + CY * x : KOWN + CY * x + CY, :]
        raw2 = weight * (slab_laplace(recv, i) / alpha)
        raw2_out[i] = raw2
        squares = squares + raw2 * raw2
        field[i + 1] = weight * raw2
    contrib = products_t(raw1, blocks, r_hot[...])
    send[:, 0:CAP, :] = onehot_dot(p_hot[...], contrib, 1, 0).reshape(RAY, CAP, LANES)
    low, high = [], []
    for x in range(CX):
        at = tile * CX + x + 1
        f = field[at]
        beside = row_sides(f, 0.0, 0.0) + lane_sides(f) + field[at - 1] + field[at + 1]
        nq_out[CY * x : CY * x + CY, :] = 6.0 * f - beside
        low.append(f[0:1])
        high.append(f[CY - 1 : CY])
    send_edges(send, None, scratch, low, high, total(raw1 * raw1) + total(squares), ray)


def kernel_next_v(pos_ref, recv, q_ref, v0_raw, alpha0, nq, send, v_out, beta_out, scratch):
    ray = pos_ref[0]
    contrib = recv[:, 0:CAP, :].reshape(RAY * CAP, LANES)
    q_hot = q_ref[...]
    norm = recv[0, MSG - 1 : MSG, :]
    for d in range(1, RAY):
        norm = norm + recv[d, MSG - 1 : MSG, :]
    beta = jnp.sqrt(norm + eps)
    beta_out[...] = beta
    z = onehot_dot(q_hot, contrib, 0, 0)
    low = jnp.where(ray > 0, recv[jnp.maximum(ray - 1, 0), CAP:MSG, :], 0.0)
    high = jnp.where(ray < RAY - 1, recv[jnp.minimum(ray + 1, RAY - 1), CAP:MSG, :], 0.0)
    row = iota((CY, LANES), 0)
    squares = jnp.zeros((CY, LANES), F32)
    edges_low, edges_high, parts = [], [], []
    for x in range(CX):
        cut = slice(CY * x, CY * x + CY)
        edge = jnp.where(row == 0, low[x : x + 1], 0.0) + jnp.where(row == CY - 1, high[x : x + 1], 0.0)
        v_raw = (z[cut] + (nq[cut, :] - edge)) / beta - beta * (v0_raw[cut, :] / alpha0[...])
        parts.append(v_raw)
        squares = squares + v_raw * v_raw
        edges_low.append(v_raw[0:1])
        edges_high.append(v_raw[CY - 1 : CY])
    v_raw = jnp.concatenate(parts, axis=0)
    v_out[...] = v_raw
    spread(send, q_hot, jnp.concatenate([v_raw, jnp.zeros((LANES - CELLS, LANES), F32)], axis=0))
    send_edges(send, None, scratch, edges_low, edges_high, total(squares), ray)


def kernel_last_norm(pos_ref, recv, start, beta1, raw1_ref, raw2_ref, send, raw1_out, alpha_out, scratch):
    tile = pos_ref[1]
    kv, alpha = gathered(recv)
    alpha_out[...] = alpha
    raw1 = kv / alpha - alpha * (raw1_ref[...] / beta1[...])
    scratch[...] = raw1.reshape(TILE, KOWN, LANES)
    raw1_out[...] = scratch[tile]
    squares = jnp.zeros((CY, LANES), F32)
    for i in range(TILE * CX):
        t, x = divmod(i, CX)
        weight = start[t, KOWN + CY * x : KOWN + CY * x + CY, :]
        raw2 = weight * (slab_laplace(recv, i) / alpha) - alpha * (raw2_ref[i] / beta1[...])
        squares = squares + raw2 * raw2
    norm = total(raw1 * raw1) + total(squares)
    send[...] = jnp.broadcast_to(norm.reshape(1, 1, 1), (RAY, 1, LANES))


def kernel_end(recv, v0_raw, v1_raw, raw1, beta0, beta1, alpha0, alpha1, model_out, u_out):
    norm = recv[0]
    for d in range(1, RAY):
        norm = norm + recv[d]
    b0, b1, b2 = beta0[...], beta1[...], jnp.sqrt(norm + eps)
    a0, a1 = alpha0[...], alpha1[...]
    v0, v1 = v0_raw[...] / a0, v1_raw[...] / a1
    rho1 = jnp.sqrt(a0 * a0 + b1 * b1)
    cosine1, sine1 = a0 / rho1, b1 / rho1
    theta = sine1 * a1
    rhobar = -cosine1 * a1
    phi1, phibar = cosine1 * b0, sine1 * b0
    w1 = v1 - theta / rho1 * v0
    rho2 = jnp.sqrt(rhobar * rhobar + b2 * b2)
    phi2 = rhobar / rho2 * phibar
    model_out[...] = phi1 / rho1 * v0 + phi2 / rho2 * w1
    u_out[...] = raw1[...] / b2


VM = pl.BlockSpec(memory_space=pltpu.VMEM)
SM = pl.BlockSpec(memory_space=pltpu.SMEM)


def call(kernel, outs, args, specs=None, scratch=()):
    return pl.pallas_call(
        kernel,
        out_shape=[jax.ShapeDtypeStruct(shape, kind) for shape, kind in outs],
        in_specs=specs or [VM] * len(args),
        out_specs=[VM] * len(outs),
        scratch_shapes=[pltpu.VMEM(shape, F32) for shape in scratch],
        compiler_params=pltpu.CompilerParams(vmem_limit_bytes=32 * 2**20),
        name=kernel.__name__,
    )(*args)


def shards(data, blocks, block_cols, block_rows, block_counts, reg_weight):
    pos = jnp.stack([lax.axis_index("ray"), lax.axis_index("tile")]).astype(jnp.int32)
    values = blocks[0, 0]
    own = jnp.concatenate([data.reshape(KOWN, LANES), reg_weight.reshape(CELLS, LANES)], axis=0)
    start = lax.all_to_all(jnp.broadcast_to(own, (TILE,) + own.shape), "tile", 0, 0)
    message = ((RAY, MSG, LANES), F32)
    tile_message = ((TILE, TMSG, LANES), F32)
    scalar = ((1, LANES), F32)
    cells = ((CELLS, LANES), F32)
    edges = (2, 8, LANES)
    send, p_hot, r_hot = call(
        kernel_start,
        [message, ((RAY * CAP, SLOTS), BF16), ((KB, SLOTS), BF16)],
        (pos, start, block_cols[0], block_rows[0], block_counts, values),
        [SM, VM, VM, VM, SM, VM],
    )
    recv = lax.all_to_all(send, "ray", 0, 0)
    send, v0_raw, q_hot, beta0 = call(
        kernel_first_v,
        [message, cells, ((RAY * CAP, LANES), BF16), scalar],
        (pos, recv),
        [SM, VM],
        [edges],
    )
    recv = lax.all_to_all(send, "ray", 0, 0)
    (send,) = call(
        kernel_forward, [tile_message], (pos, recv, p_hot, r_hot, values, v0_raw), [SM] + [VM] * 5
    )
    recv = lax.all_to_all(send, "tile", 0, 0)
    send, raw1, raw2, alpha0, nq = call(
        kernel_back,
        [message, ((KB, LANES), F32), ((TILE * CX, CY, LANES), F32), scalar, cells],
        (pos, recv, start, beta0, values, p_hot, r_hot),
        [SM] + [VM] * 6,
        [edges, (TILE * CX + 2, CY, LANES)],
    )
    recv = lax.all_to_all(send, "ray", 0, 0)
    send, v1_raw, beta1 = call(
        kernel_next_v,
        [message, cells, scalar],
        (pos, recv, q_hot, v0_raw, alpha0, nq),
        [SM] + [VM] * 5,
        [edges],
    )
    recv = lax.all_to_all(send, "ray", 0, 0)
    (send,) = call(
        kernel_forward, [tile_message], (pos, recv, p_hot, r_hot, values, v1_raw), [SM] + [VM] * 5
    )
    recv = lax.all_to_all(send, "tile", 0, 0)
    send, raw1_own, alpha1 = call(
        kernel_last_norm,
        [((RAY, 1, LANES), F32), ((KOWN, LANES), F32), scalar],
        (pos, recv, start, beta1, raw1, raw2),
        [SM] + [VM] * 5,
        [(TILE, KOWN, LANES)],
    )
    recv = lax.all_to_all(send, "ray", 0, 0)
    model, rays = call(
        kernel_end,
        [cells, ((KOWN, LANES), F32)],
        (recv, v0_raw, v1_raw, raw1_own, beta0, beta1, alpha0, alpha1),
    )
    return model.reshape(reg_weight.shape), rays.reshape(data.shape)


def solution(mesh):
    return jax.shard_map(
        shards,
        mesh=mesh,
        in_specs=(
            P(("ray", "tile")),
            P("ray", "tile", None, None, None),
            P("ray", "tile", None),
            P("ray", "tile", None),
            P("ray", "tile"),
            P("tile", "ray", None),
        ),
        out_specs=(P("tile", "ray", None), P(("ray", "tile"))),
        check_vma=False,
    )
```

```python
import jax
import jax.numpy as jnp
from jax import lax
from jax.experimental import pallas as pl
from jax.experimental.pallas import tpu as pltpu
from jax.sharding import PartitionSpec as P

RAY = 32
TILE = 8
CAP = 8
CX = 4
CY = 8
CELLS = CX * CY
SLOTS = 128
LANES = 128
KB = 64
KOWN = KB // TILE
MSG = 2 * CAP
TMSG = KB + CELLS + 16
SMSG = KOWN + CELLS
XS = TILE * CX
eps = 1e-06

F32 = jnp.float32
BF16 = jnp.bfloat16


def iota(shape, dim):
    return lax.broadcasted_iota(jnp.int32, shape, dim)


def dot(a, b, ca, cb):
    return lax.dot_general(a, b, (((ca,), (cb,)), ((), ())), preferred_element_type=F32)


def onehot_dot(hot, x, ca, cb):
    high = x.astype(BF16)
    rest = x - high.astype(F32)
    mid = rest.astype(BF16)
    low = (rest - mid.astype(F32)).astype(BF16)
    return dot(hot, high, ca, cb) + (dot(hot, mid, ca, cb) + dot(hot, low, ca, cb))


def total(x):
    return jnp.sum(jnp.sum(x, axis=0, keepdims=True), axis=1, keepdims=True)


def terms(x):
    high = x.astype(BF16).astype(F32)
    mid = (x - high).astype(BF16).astype(F32)
    return high, mid, x - high - mid


def wide(x):
    return jnp.broadcast_to(x, (1, LANES))


def lane_sides(f):
    lane = iota(f.shape, 1)
    left = jnp.where(lane == 0, 0.0, pltpu.roll(f, 1, 1))
    right = jnp.where(lane == LANES - 1, 0.0, pltpu.roll(f, LANES - 1, 1))
    return left + right


def row_sides(f, low, high):
    row = iota(f.shape, 0)
    below = jnp.where(row == 0, low, pltpu.roll(f, 1, 0))
    above = jnp.where(row == CY - 1, high, pltpu.roll(f, CY - 1, 0))
    return below + above


def products_t(picked, blocks, first):
    row = iota((8, LANES), 0)
    out = []
    for q in range(picked.shape[0] // 8):
        p = picked[8 * q : 8 * q + 8, :]
        lhs = jnp.concatenate([jnp.where(row == i, p, 0.0) for i in range(8)], axis=1)
        at = first + 8 * q
        out.append(dot(lhs.astype(BF16), blocks[at : at + 8].reshape(8 * LANES, LANES), 1, 0))
    return jnp.concatenate(out, axis=0)


def products(x, blocks, r_hot):
    row = iota((8, LANES), 0)
    out = []
    for q in range(SLOTS // 8):
        p = x[8 * q : 8 * q + 8, :]
        lhs = jnp.concatenate([jnp.where(row == i, p, 0.0) for i in range(8)], axis=1)
        rhs = jnp.concatenate([blocks[8 * q + i] for i in range(8)], axis=1)
        out.append(dot(lhs.astype(BF16), rhs, 1, 1))
    return onehot_dot(r_hot, jnp.concatenate(out, axis=0), 1, 0)


def edge_tiles(scratch, low, high, scalar):
    for x in range(CX):
        scratch[0, x : x + 1, :] = low[x]
        scratch[1, x : x + 1, :] = high[x]
    for i, term in enumerate(terms(scalar)):
        scratch[0, CX + i : CX + i + 1, :] = wide(term)
        scratch[1, CX + i : CX + i + 1, :] = wide(term)
    scratch[0, 7:8, :] = jnp.zeros((1, LANES), F32)
    scratch[1, 7:8, :] = jnp.zeros((1, LANES), F32)
    return scratch[0], scratch[1]


def kernel_index(cols, rows, count, p_out, p_wide_out, r_out, note_out):
    col = cols[...]
    live = iota((1, SLOTS), 1) < count[...]
    slab = RAY * CY
    owner = lax.div(lax.rem(col, slab), CY)
    local = lax.div(col, slab) * CY + lax.rem(col, CY)
    own_hot = iota((RAY, SLOTS), 0) == owner
    before = (iota((SLOTS, SLOTS), 0) < iota((SLOTS, SLOTS), 1)).astype(F32).astype(BF16)
    earlier = dot(own_hot.astype(F32).astype(BF16), before, 1, 0)
    rank = jnp.sum(jnp.where(own_hot, earlier, 0.0), axis=0, keepdims=True).astype(jnp.int32)
    p_f = ((iota((RAY * CAP, SLOTS), 0) == owner * CAP + rank) & live).astype(F32)
    p_out[...] = p_f.astype(BF16)
    p_wide_out[...] = ((iota((RAY * MSG, SLOTS), 0) == owner * MSG + rank) & live).astype(F32).astype(BF16)
    r_out[...] = ((iota((KB, SLOTS), 0) == rows[...]) & live).astype(F32).astype(BF16)
    ids = jnp.sum(p_f * (local + 1).astype(F32), axis=1, keepdims=True) - 1.0
    note_out[...] = jnp.broadcast_to(ids, (RAY * CAP, LANES))


def kernel_start(pos_ref, start, note, blocks, p_hot, r_hot, send):
    data = start[:, 0:KOWN, :].reshape(KB, LANES)
    contrib = products_t(dot(r_hot[...], data.astype(BF16), 0, 0), blocks, 0)
    send[:, 0:CAP, :] = onehot_dot(p_hot[...], contrib, 1, 0).reshape(RAY, CAP, LANES)
    lane = iota((RAY * CAP, LANES), 1)
    send[:, CAP:MSG, :] = jnp.where(lane < LANES // 2, note[...], total(data * data)).reshape(RAY, CAP, LANES)


def send_columns(send, q_hot, v_raw, scratch, low, high, scalar, ray):
    columns = dot(q_hot, v_raw.astype(BF16), 1, 0)
    low, high = edge_tiles(scratch, low, high, scalar)
    for d in range(RAY):
        edge = jnp.where(d > ray, high, low)
        send[d] = jnp.concatenate([columns[CAP * d : CAP * d + CAP], edge], axis=0).astype(BF16)


def kernel_first_v(pos_ref, recv, send, v_out, q_out, beta_out, scratch):
    contrib = recv[:, 0:CAP, :].reshape(RAY * CAP, LANES)
    note = recv[:, CAP:MSG, :].reshape(RAY * CAP, LANES)
    lane = iota((RAY * CAP, LANES), 1)
    row = iota((RAY * CAP, LANES), 0)
    q_hot = (note[:, 0:CELLS] == iota((RAY * CAP, CELLS), 1).astype(F32)).astype(F32).astype(BF16)
    q_out[...] = q_hot
    squares = total(jnp.where((lane == LANES - 1) & (lax.rem(row, CAP) == 0), note, 0.0))
    beta = jnp.sqrt(squares + eps)
    beta_out[...] = wide(beta)
    v_raw = onehot_dot(q_hot, contrib, 0, 0) / beta
    v_out[...] = v_raw
    low = [v_raw[CY * x : CY * x + 1, :] for x in range(CX)]
    high = [v_raw[CY * x + CY - 1 : CY * x + CY, :] for x in range(CX)]
    send_columns(send, q_hot, v_raw, scratch, low, high, total(v_raw * v_raw), pos_ref[0])


def kernel_forward(pos_ref, recv, p_wide, r_hot, blocks, v_raw, send, scratch):
    ray = pos_ref[0]
    x = dot(p_wide[...], recv[...].reshape(RAY * MSG, LANES), 0, 0)
    part = products(x, blocks, r_hot[...]).astype(BF16)
    norm = jnp.zeros((MSG, LANES), F32)
    for d in range(RAY):
        norm = norm + recv[d].astype(F32)
    low = recv[jnp.maximum(ray - 1, 0)].astype(F32)
    high = recv[jnp.minimum(ray + 1, RAY - 1)].astype(F32)
    scratch[0:CX, :] = jnp.where(ray > 0, low[CAP : CAP + CX], 0.0)
    scratch[CX : 2 * CX, :] = jnp.where(ray < RAY - 1, high[CAP : CAP + CX], 0.0)
    at = CAP + CX
    norm = norm[at : at + 1] + (norm[at + 1 : at + 2] + norm[at + 2 : at + 3])
    for i, term in enumerate(terms(norm)):
        scratch[2 * CX + i : 2 * CX + i + 1, :] = term
    scratch[2 * CX + 3 : 16, :] = jnp.zeros((16 - 2 * CX - 3, LANES), F32)
    edge = scratch[...].astype(BF16)
    mine = v_raw[...].astype(BF16)
    for t in range(TILE):
        send[t, 0:KB, :] = part
        send[t, KB : KB + CELLS, :] = mine
        send[t, KB + CELLS : TMSG, :] = edge


def gathered(recv, v_raw, tile, slab, edges):
    kv = recv[0, 0:KB, :].astype(F32)
    for t in range(1, TILE):
        kv = kv + recv[t, 0:KB, :].astype(F32)
    slab[0] = jnp.zeros((CY, LANES), F32)
    slab[XS + 1] = jnp.zeros((CY, LANES), F32)
    norm = jnp.zeros((8, LANES), F32)
    for t in range(TILE):
        for h in range(CELLS // 16):
            both = recv[t, KB + 16 * h : KB + 16 * h + 16, :].astype(F32)
            slab[CX * t + 2 * h + 1] = both[0:CY]
            slab[CX * t + 2 * h + 2] = both[CY : 2 * CY]
        edge = recv[t, KB + CELLS : TMSG, :].astype(F32)
        edges[t] = edge[0:8]
        norm = norm + edge[8:16]
    for x in range(CX):
        slab[CX * tile + x + 1] = v_raw[CY * x : CY * x + CY, :]
    return kv, jnp.sqrt(norm[0:1] + (norm[1:2] + norm[2:3]) + eps)


def slab_laplace(slab, edges, index):
    t, x = divmod(index, CX)
    f = slab[index + 1]
    beside = row_sides(f, edges[t, x : x + 1, :], edges[t, CX + x : CX + x + 1, :])
    beside = beside + lane_sides(f) + slab[index] + slab[index + 2]
    return 6.0 * f - beside


def cell_weight(start, index):
    t, x = divmod(index, CX)
    return start[t, KOWN + CY * x : KOWN + CY * x + CY, :]


def kernel_back(
    pos_ref, recv, v_raw, start, beta0, blocks, p_hot, r_hot,
    send, raw1_out, raw2_out, alpha_out, nq_out,
    scratch, slab, edges, field,
):
    ray, tile = pos_ref[0], pos_ref[1]
    kv, alpha = gathered(recv, v_raw, tile, slab, edges)
    alpha_out[...] = alpha
    raw1 = kv / alpha - alpha * (start[:, 0:KOWN, :].reshape(KB, LANES) / beta0[...])
    raw1_out[...] = raw1
    field[0] = jnp.zeros((CY, LANES), F32)
    field[XS + 1] = jnp.zeros((CY, LANES), F32)
    squares = jnp.zeros((CY, LANES), F32)
    for i in range(XS):
        weight = cell_weight(start, i)
        raw2 = weight * (slab_laplace(slab, edges, i) / alpha)
        raw2_out[i] = raw2
        squares = squares + raw2 * raw2
        field[i + 1] = weight * raw2
    contrib = products_t(dot(r_hot[...], raw1.astype(BF16), 0, 0), blocks, 0)
    send[:, 0:CAP, :] = onehot_dot(p_hot[...], contrib, 1, 0).reshape(RAY, CAP, LANES)
    low, high = [], []
    for x in range(CX):
        at = tile * CX + x + 1
        f = field[at]
        beside = row_sides(f, 0.0, 0.0) + lane_sides(f) + field[at - 1] + field[at + 1]
        nq_out[CY * x : CY * x + CY, :] = 6.0 * f - beside
        low.append(f[0:1])
        high.append(f[CY - 1 : CY])
    low, high = edge_tiles(scratch, low, high, total(raw1 * raw1) + total(squares))
    for d in range(RAY):
        send[d, CAP:MSG, :] = jnp.where(d > ray, high, low)


def kernel_next_v(pos_ref, recv, q_ref, v0_raw, alpha0, nq, send, v_out, beta_out, scratch):
    ray = pos_ref[0]
    contrib = recv[:, 0:CAP, :].reshape(RAY * CAP, LANES)
    q_hot = q_ref[...]
    norm = recv[0, CAP:MSG, :]
    for d in range(1, RAY):
        norm = norm + recv[d, CAP:MSG, :]
    beta = jnp.sqrt(norm[CX : CX + 1] + (norm[CX + 1 : CX + 2] + norm[CX + 2 : CX + 3]) + eps)
    beta_out[...] = beta
    z = onehot_dot(q_hot, contrib, 0, 0)
    low = jnp.where(ray > 0, recv[jnp.maximum(ray - 1, 0), CAP:MSG, :], 0.0)
    high = jnp.where(ray < RAY - 1, recv[jnp.minimum(ray + 1, RAY - 1), CAP:MSG, :], 0.0)
    row = iota((CY, LANES), 0)
    squares = jnp.zeros((CY, LANES), F32)
    edges_low, edges_high, parts = [], [], []
    for x in range(CX):
        cut = slice(CY * x, CY * x + CY)
        edge = jnp.where(row == 0, low[x : x + 1], 0.0) + jnp.where(row == CY - 1, high[x : x + 1], 0.0)
        v_raw = (z[cut] + (nq[cut, :] - edge)) / beta - beta * (v0_raw[cut, :] / alpha0[...])
        v_out[cut, :] = v_raw
        parts.append(v_raw)
        squares = squares + v_raw * v_raw
        edges_low.append(v_raw[0:1])
        edges_high.append(v_raw[CY - 1 : CY])
    send_columns(send, q_hot, jnp.concatenate(parts, axis=0), scratch, edges_low, edges_high, total(squares), ray)


def kernel_last_norm(
    pos_ref, recv, v_raw, start, beta1, raw1_ref, raw2_ref, send, raw1_out, alpha_out, scratch, slab, edges
):
    tile = pos_ref[1]
    kv, alpha = gathered(recv, v_raw, tile, slab, edges)
    alpha_out[...] = alpha
    raw1 = kv / alpha - alpha * (raw1_ref[...] / beta1[...])
    scratch[...] = raw1.reshape(TILE, KOWN, LANES)
    raw1_out[...] = scratch[tile]
    squares = jnp.zeros((CY, LANES), F32)
    for i in range(XS):
        raw2 = cell_weight(start, i) * (slab_laplace(slab, edges, i) / alpha) - alpha * (raw2_ref[i] / beta1[...])
        squares = squares + raw2 * raw2
    norm = total(raw1 * raw1) + total(squares)
    send[...] = jnp.broadcast_to(norm.reshape(1, 1, 1), (RAY, 1, LANES))


def kernel_end(recv, v0_raw, v1_raw, raw1, beta0, beta1, alpha0, alpha1, model_out, u_out):
    norm = recv[0]
    for d in range(1, RAY):
        norm = norm + recv[d]
    b0, b1, b2 = beta0[...], beta1[...], jnp.sqrt(norm + eps)
    a0, a1 = alpha0[...], alpha1[...]
    v0, v1 = v0_raw[...] / a0, v1_raw[...] / a1
    rho1 = jnp.sqrt(a0 * a0 + b1 * b1)
    cosine1, sine1 = a0 / rho1, b1 / rho1
    theta = sine1 * a1
    rhobar = -cosine1 * a1
    phi1, phibar = cosine1 * b0, sine1 * b0
    w1 = v1 - theta / rho1 * v0
    rho2 = jnp.sqrt(rhobar * rhobar + b2 * b2)
    phi2 = rhobar / rho2 * phibar
    model_out[...] = phi1 / rho1 * v0 + phi2 / rho2 * w1
    u_out[...] = raw1[...] / b2


VM = pl.BlockSpec(memory_space=pltpu.VMEM)
SM = pl.BlockSpec(memory_space=pltpu.SMEM)


def call(kernel, outs, args, specs=None, scratch=()):
    return pl.pallas_call(
        kernel,
        out_shape=[jax.ShapeDtypeStruct(shape, kind) for shape, kind in outs],
        in_specs=specs or [SM] + [VM] * (len(args) - 1),
        out_specs=[VM] * len(outs),
        scratch_shapes=[pltpu.VMEM(s, F32) if isinstance(s, tuple) else s for s in scratch],
        compiler_params=pltpu.CompilerParams(vmem_limit_bytes=32 * 2**20),
        name=kernel.__name__,
    )(*args)


def shards(data, blocks, block_cols, block_rows, block_counts, reg_weight):
    pos = jnp.stack([lax.axis_index("ray"), lax.axis_index("tile")]).astype(jnp.int32)
    weight = reg_weight.reshape(CELLS, LANES)
    message = ((RAY, MSG, LANES), F32)
    half_message = ((RAY, MSG, LANES), BF16)
    tile_message = ((TILE, TMSG, LANES), BF16)
    scalar = ((1, LANES), F32)
    cells = ((CELLS, LANES), F32)
    rays = ((KB, LANES), F32)
    slab = ((XS, CY, LANES), F32)
    edges = (2, 8, LANES)
    slabs = [(XS + 2, CY, LANES), (TILE, 8, LANES)]
    own = jnp.concatenate([data.reshape(KOWN, LANES), weight], axis=0)
    start = lax.all_to_all(jnp.broadcast_to(own, (TILE,) + own.shape), "tile", 0, 0)
    p_hot, p_wide, r_hot, note = call(
        kernel_index,
        [
            ((RAY * CAP, SLOTS), BF16),
            ((RAY * MSG, SLOTS), BF16),
            ((KB, SLOTS), BF16),
            ((RAY * CAP, LANES), F32),
        ],
        (block_cols[0], block_rows[0], block_counts),
        [VM] * 3,
    )
    values = blocks[0, 0]
    (send,) = call(kernel_start, [message], (pos, start, note, values, p_hot, r_hot))
    recv = lax.all_to_all(send, "ray", 0, 0)
    send, v0_raw, q_hot, beta0 = call(
        kernel_first_v,
        [half_message, cells, ((RAY * CAP, CELLS), BF16), scalar],
        (pos, recv),
        scratch=[edges],
    )
    recv = lax.all_to_all(send, "ray", 0, 0)
    (send,) = call(
        kernel_forward, [tile_message], (pos, recv, p_wide, r_hot, values, v0_raw), scratch=[(16, LANES)]
    )
    recv = lax.all_to_all(send, "tile", 0, 0)
    send, raw1, raw2, alpha0, nq = call(
        kernel_back,
        [message, rays, slab, scalar, cells],
        (pos, recv, v0_raw, start, beta0, values, p_hot, r_hot),
        scratch=[edges] + slabs + slabs[:1],
    )
    recv = lax.all_to_all(send, "ray", 0, 0)
    send, v1_raw, beta1 = call(
        kernel_next_v,
        [half_message, cells, scalar],
        (pos, recv, q_hot, v0_raw, alpha0, nq),
        scratch=[edges],
    )
    recv = lax.all_to_all(send, "ray", 0, 0)
    (send,) = call(
        kernel_forward, [tile_message], (pos, recv, p_wide, r_hot, values, v1_raw), scratch=[(16, LANES)]
    )
    recv = lax.all_to_all(send, "tile", 0, 0)
    send, raw1_own, alpha1 = call(
        kernel_last_norm,
        [((RAY, 1, LANES), F32), ((KOWN, LANES), F32), scalar],
        (pos, recv, v1_raw, start, beta1, raw1, raw2),
        scratch=[(TILE, KOWN, LANES)] + slabs,
    )
    recv = lax.all_to_all(send, "ray", 0, 0)
    model, rays = call(
        kernel_end,
        [cells, ((KOWN, LANES), F32)],
        (recv, v0_raw, v1_raw, raw1_own, beta0, beta1, alpha0, alpha1),
        [VM] * 8,
    )
    return model.reshape(reg_weight.shape), rays.reshape(data.shape)


def solution(mesh):
    return jax.shard_map(
        shards,
        mesh=mesh,
        in_specs=(
            P(("ray", "tile")),
            P("ray", "tile", None, None, None),
            P("ray", "tile", None),
            P("ray", "tile", None),
            P("ray", "tile"),
            P("tile", "ray", None),
        ),
        out_specs=(P("tile", "ray", None), P(("ray", "tile"))),
        check_vma=False,
    )
```

```python
import jax
import jax.numpy as jnp
from jax import lax
from jax.experimental import pallas as pl
from jax.experimental.pallas import tpu as pltpu
from jax.sharding import PartitionSpec as P

RAY = 32
TILE = 8
CAP = 8
CX = 4
CY = 8
CELLS = CX * CY
SLOTS = 128
LANES = 128
KB = 64
KOWN = KB // TILE
MSG = 2 * CAP
TMSG = KB + CELLS + 16
SMSG = KOWN + CELLS
CHUNKS = 4
XS = TILE * CX
eps = 1e-06

F32 = jnp.float32
BF16 = jnp.bfloat16


def iota(shape, dim):
    return lax.broadcasted_iota(jnp.int32, shape, dim)


def dot(a, b, ca, cb):
    return lax.dot_general(a, b, (((ca,), (cb,)), ((), ())), preferred_element_type=F32)


def onehot_dot(hot, x, ca, cb):
    high = x.astype(BF16)
    rest = x - high.astype(F32)
    mid = rest.astype(BF16)
    low = (rest - mid.astype(F32)).astype(BF16)
    return dot(hot, high, ca, cb) + (dot(hot, mid, ca, cb) + dot(hot, low, ca, cb))


def total(x):
    return jnp.sum(jnp.sum(x, axis=0, keepdims=True), axis=1, keepdims=True)


def terms(x):
    high = x.astype(BF16).astype(F32)
    mid = (x - high).astype(BF16).astype(F32)
    return high, mid, x - high - mid


def wide(x):
    return jnp.broadcast_to(x, (1, LANES))


def lane_sides(f):
    lane = iota(f.shape, 1)
    left = jnp.where(lane == 0, 0.0, pltpu.roll(f, 1, 1))
    right = jnp.where(lane == LANES - 1, 0.0, pltpu.roll(f, LANES - 1, 1))
    return left + right


def row_sides(f, low, high):
    row = iota(f.shape, 0)
    below = jnp.where(row == 0, low, pltpu.roll(f, 1, 0))
    above = jnp.where(row == CY - 1, high, pltpu.roll(f, CY - 1, 0))
    return below + above


def products_t(picked, blocks, first):
    row = iota((8, LANES), 0)
    out = []
    for q in range(picked.shape[0] // 8):
        p = picked[8 * q : 8 * q + 8, :]
        lhs = jnp.concatenate([jnp.where(row == i, p, 0.0) for i in range(8)], axis=1)
        at = first + 8 * q
        out.append(dot(lhs.astype(BF16), blocks[at : at + 8].reshape(8 * LANES, LANES), 1, 0))
    return jnp.concatenate(out, axis=0)


def products(x, blocks, r_hot):
    row = iota((8, LANES), 0)
    out = []
    for q in range(SLOTS // 8):
        p = x[8 * q : 8 * q + 8, :]
        lhs = jnp.concatenate([jnp.where(row == i, p, 0.0) for i in range(8)], axis=1)
        rhs = jnp.concatenate([blocks[8 * q + i] for i in range(8)], axis=1)
        out.append(dot(lhs.astype(BF16), rhs, 1, 1))
    return onehot_dot(r_hot, jnp.concatenate(out, axis=0), 1, 0)


def edge_tiles(scratch, low, high, scalar):
    for x in range(CX):
        scratch[0, x : x + 1, :] = low[x]
        scratch[1, x : x + 1, :] = high[x]
    for i, term in enumerate(terms(scalar)):
        scratch[0, CX + i : CX + i + 1, :] = wide(term)
        scratch[1, CX + i : CX + i + 1, :] = wide(term)
    scratch[0, 7:8, :] = jnp.zeros((1, LANES), F32)
    scratch[1, 7:8, :] = jnp.zeros((1, LANES), F32)
    return scratch[0], scratch[1]


def kernel_index(cols, rows, count, p_out, p_wide_out, r_out, r_turned_out, note_out):
    col = cols[...]
    live = iota((1, SLOTS), 1) < count[...]
    slab = RAY * CY
    owner = lax.div(lax.rem(col, slab), CY)
    local = lax.div(col, slab) * CY + lax.rem(col, CY)
    own_hot = iota((RAY, SLOTS), 0) == owner
    before = (iota((SLOTS, SLOTS), 0) < iota((SLOTS, SLOTS), 1)).astype(F32).astype(BF16)
    earlier = dot(own_hot.astype(F32).astype(BF16), before, 1, 0)
    rank = jnp.sum(jnp.where(own_hot, earlier, 0.0), axis=0, keepdims=True).astype(jnp.int32)
    p_f = ((iota((RAY * CAP, SLOTS), 0) == owner * CAP + rank) & live).astype(F32)
    p_out[...] = p_f.astype(BF16)
    p_wide = ((iota((RAY * MSG, SLOTS), 0) == owner * MSG + rank) & live).astype(F32)
    p_wide_out[...] = p_wide.T.astype(BF16)
    r_f = ((iota((KB, SLOTS), 0) == rows[...]) & live).astype(F32)
    r_out[...] = r_f.astype(BF16)
    r_turned_out[...] = r_f.T.astype(BF16)
    ids = jnp.sum(p_f * (local + 1).astype(F32), axis=1, keepdims=True) - 1.0
    note_out[...] = jnp.broadcast_to(ids, (RAY * CAP, LANES))


def send_contributions(send, p_hot, contrib, notes):
    slots = dot(p_hot, contrib.astype(BF16), 1, 0)
    for d in range(RAY):
        send[d] = jnp.concatenate([slots[CAP * d : CAP * d + CAP], notes(d)], axis=0).astype(BF16)


def received(recv):
    both = [recv[d].astype(F32) for d in range(RAY)]
    contrib = jnp.concatenate([x[0:CAP] for x in both], axis=0).astype(BF16)
    return contrib, [x[CAP:MSG] for x in both]


def kernel_start(pos_ref, start, note, blocks, p_hot, r_turned, send, held, sems):
    per = SLOTS // CHUNKS
    copies = [
        pltpu.make_async_copy(blocks.at[pl.ds(c * per, per)], held.at[pl.ds(c * per, per)], sems.at[c])
        for c in range(CHUNKS)
    ]
    for copy in copies:
        copy.start()
    data = start[:, 0:KOWN, :].reshape(KB, LANES)
    picked = dot(r_turned[...], data.astype(BF16), 1, 0)
    contrib = []
    for c, copy in enumerate(copies):
        copy.wait()
        contrib.append(products_t(picked[c * per : (c + 1) * per], held, c * per))
    contrib = jnp.concatenate(contrib, axis=0)
    quarter = iota((CAP, LANES), 1) // CELLS
    high, mid, low = terms(total(data * data))
    squares = jnp.where(quarter == 1, high, jnp.where(quarter == 2, mid, low))
    send_contributions(
        send, p_hot[...], contrib,
        lambda d: jnp.where(quarter == 0, note[CAP * d : CAP * d + CAP, :], squares),
    )


def send_columns(send, q_hot, v_raw, scratch, low, high, scalar, ray):
    columns = dot(q_hot, v_raw.astype(BF16), 1, 0)
    low, high = edge_tiles(scratch, low, high, scalar)
    for d in range(RAY):
        edge = jnp.where(d > ray, high, low)
        send[d] = jnp.concatenate([columns[CAP * d : CAP * d + CAP], edge], axis=0).astype(BF16)


def kernel_first_v(pos_ref, recv, send, v_out, q_out, beta_out, scratch):
    contrib, notes = received(recv)
    norm = notes[0][0:1]
    for d in range(1, RAY):
        norm = norm + notes[d][0:1]
    note = jnp.concatenate(notes, axis=0)
    q_hot = (note[:, 0:CELLS] == iota((RAY * CAP, CELLS), 1).astype(F32)).astype(F32).astype(BF16)
    q_out[...] = q_hot
    lane = iota((1, LANES), 1)
    squares = total(jnp.where((lane > 0) & (lane % CELLS == 0), norm, 0.0))
    beta = jnp.sqrt(squares + eps)
    beta_out[...] = wide(beta)
    v_raw = dot(q_hot, contrib, 0, 0) / beta
    v_out[...] = v_raw
    low = [v_raw[CY * x : CY * x + 1, :] for x in range(CX)]
    high = [v_raw[CY * x + CY - 1 : CY * x + CY, :] for x in range(CX)]
    send_columns(send, q_hot, v_raw, scratch, low, high, total(v_raw * v_raw), pos_ref[0])


def kernel_forward(pos_ref, recv, p_wide, r_hot, blocks, v_raw, send, scratch):
    ray = pos_ref[0]
    x = dot(p_wide[...], recv[...].reshape(RAY * MSG, LANES), 1, 0)
    part = products(x, blocks, r_hot[...]).astype(BF16)
    norm = jnp.zeros((MSG, LANES), F32)
    for d in range(RAY):
        norm = norm + recv[d].astype(F32)
    low = recv[jnp.maximum(ray - 1, 0)].astype(F32)
    high = recv[jnp.minimum(ray + 1, RAY - 1)].astype(F32)
    scratch[0:CX, :] = jnp.where(ray > 0, low[CAP : CAP + CX], 0.0)
    scratch[CX : 2 * CX, :] = jnp.where(ray < RAY - 1, high[CAP : CAP + CX], 0.0)
    at = CAP + CX
    norm = norm[at : at + 1] + (norm[at + 1 : at + 2] + norm[at + 2 : at + 3])
    for i, term in enumerate(terms(norm)):
        scratch[2 * CX + i : 2 * CX + i + 1, :] = term
    scratch[2 * CX + 3 : 16, :] = jnp.zeros((16 - 2 * CX - 3, LANES), F32)
    edge = scratch[...].astype(BF16)
    mine = v_raw[...].astype(BF16)
    for t in range(TILE):
        send[t, 0:KB, :] = part
        send[t, KB : KB + CELLS, :] = mine
        send[t, KB + CELLS : TMSG, :] = edge


def gathered(recv, v_raw, tile, slab, edges):
    kv = recv[0, 0:KB, :].astype(F32)
    for t in range(1, TILE):
        kv = kv + recv[t, 0:KB, :].astype(F32)
    slab[0] = jnp.zeros((CY, LANES), F32)
    slab[XS + 1] = jnp.zeros((CY, LANES), F32)
    norm = jnp.zeros((8, LANES), F32)
    for t in range(TILE):
        for h in range(CELLS // 16):
            both = recv[t, KB + 16 * h : KB + 16 * h + 16, :].astype(F32)
            slab[CX * t + 2 * h + 1] = both[0:CY]
            slab[CX * t + 2 * h + 2] = both[CY : 2 * CY]
        edge = recv[t, KB + CELLS : TMSG, :].astype(F32)
        edges[t] = edge[0:8]
        norm = norm + edge[8:16]
    for x in range(CX):
        slab[CX * tile + x + 1] = v_raw[CY * x : CY * x + CY, :]
    return kv, jnp.sqrt(norm[0:1] + (norm[1:2] + norm[2:3]) + eps)


def slab_laplace(slab, edges, index):
    t, x = divmod(index, CX)
    f = slab[index + 1]
    beside = row_sides(f, edges[t, x : x + 1, :], edges[t, CX + x : CX + x + 1, :])
    beside = beside + lane_sides(f) + slab[index] + slab[index + 2]
    return 6.0 * f - beside


def cell_weight(start, index):
    t, x = divmod(index, CX)
    return start[t, KOWN + CY * x : KOWN + CY * x + CY, :]


def kernel_back(
    pos_ref, recv, v_raw, start, beta0, blocks, p_hot, r_turned,
    send, raw1_out, raw2_out, alpha_out, nq_out,
    scratch, slab, edges, field,
):
    ray, tile = pos_ref[0], pos_ref[1]
    kv, alpha = gathered(recv, v_raw, tile, slab, edges)
    alpha_out[...] = alpha
    raw1 = kv / alpha - alpha * (start[:, 0:KOWN, :].reshape(KB, LANES) / beta0[...])
    raw1_out[...] = raw1
    field[0] = jnp.zeros((CY, LANES), F32)
    field[XS + 1] = jnp.zeros((CY, LANES), F32)
    squares = jnp.zeros((CY, LANES), F32)
    for i in range(XS):
        weight = cell_weight(start, i)
        raw2 = weight * (slab_laplace(slab, edges, i) / alpha)
        raw2_out[i] = raw2
        squares = squares + raw2 * raw2
        field[i + 1] = weight * raw2
    contrib = products_t(dot(r_turned[...], raw1.astype(BF16), 1, 0), blocks, 0)
    low, high = [], []
    for x in range(CX):
        at = tile * CX + x + 1
        f = field[at]
        beside = row_sides(f, 0.0, 0.0) + lane_sides(f) + field[at - 1] + field[at + 1]
        nq_out[CY * x : CY * x + CY, :] = 6.0 * f - beside
        low.append(f[0:1])
        high.append(f[CY - 1 : CY])
    low, high = edge_tiles(scratch, low, high, total(raw1 * raw1) + total(squares))
    send_contributions(send, p_hot[...], contrib, lambda d: jnp.where(d > ray, high, low))


def kernel_next_v(pos_ref, recv, q_ref, v0_raw, alpha0, nq, send, v_out, beta_out, scratch):
    ray = pos_ref[0]
    contrib, notes = received(recv)
    q_hot = q_ref[...]
    norm = notes[0]
    for d in range(1, RAY):
        norm = norm + notes[d]
    beta = jnp.sqrt(norm[CX : CX + 1] + (norm[CX + 1 : CX + 2] + norm[CX + 2 : CX + 3]) + eps)
    beta_out[...] = beta
    z = dot(q_hot, contrib, 0, 0)
    low = jnp.where(ray > 0, recv[jnp.maximum(ray - 1, 0)].astype(F32)[CAP:MSG], 0.0)
    high = jnp.where(ray < RAY - 1, recv[jnp.minimum(ray + 1, RAY - 1)].astype(F32)[CAP:MSG], 0.0)
    row = iota((CY, LANES), 0)
    squares = jnp.zeros((CY, LANES), F32)
    edges_low, edges_high, parts = [], [], []
    for x in range(CX):
        cut = slice(CY * x, CY * x + CY)
        edge = jnp.where(row == 0, low[x : x + 1], 0.0) + jnp.where(row == CY - 1, high[x : x + 1], 0.0)
        v_raw = (z[cut] + (nq[cut, :] - edge)) / beta - beta * (v0_raw[cut, :] / alpha0[...])
        v_out[cut, :] = v_raw
        parts.append(v_raw)
        squares = squares + v_raw * v_raw
        edges_low.append(v_raw[0:1])
        edges_high.append(v_raw[CY - 1 : CY])
    send_columns(send, q_hot, jnp.concatenate(parts, axis=0), scratch, edges_low, edges_high, total(squares), ray)


def kernel_last_norm(
    pos_ref, recv, v_raw, start, beta1, raw1_ref, raw2_ref, send, raw1_out, alpha_out, scratch, slab, edges
):
    tile = pos_ref[1]
    kv, alpha = gathered(recv, v_raw, tile, slab, edges)
    alpha_out[...] = alpha
    raw1 = kv / alpha - alpha * (raw1_ref[...] / beta1[...])
    scratch[...] = raw1.reshape(TILE, KOWN, LANES)
    raw1_out[...] = scratch[tile]
    squares = jnp.zeros((CY, LANES), F32)
    for i in range(XS):
        raw2 = cell_weight(start, i) * (slab_laplace(slab, edges, i) / alpha) - alpha * (raw2_ref[i] / beta1[...])
        squares = squares + raw2 * raw2
    norm = total(raw1 * raw1) + total(squares)
    send[...] = jnp.broadcast_to(norm.reshape(1, 1, 1), (RAY, 1, LANES))


def kernel_end(recv, v0_raw, v1_raw, raw1, beta0, beta1, alpha0, alpha1, model_out, u_out):
    norm = recv[0]
    for d in range(1, RAY):
        norm = norm + recv[d]
    b0, b1, b2 = beta0[...], beta1[...], jnp.sqrt(norm + eps)
    a0, a1 = alpha0[...], alpha1[...]
    v0, v1 = v0_raw[...] / a0, v1_raw[...] / a1
    rho1 = jnp.sqrt(a0 * a0 + b1 * b1)
    cosine1, sine1 = a0 / rho1, b1 / rho1
    theta = sine1 * a1
    rhobar = -cosine1 * a1
    phi1, phibar = cosine1 * b0, sine1 * b0
    w1 = v1 - theta / rho1 * v0
    rho2 = jnp.sqrt(rhobar * rhobar + b2 * b2)
    phi2 = rhobar / rho2 * phibar
    model_out[...] = phi1 / rho1 * v0 + phi2 / rho2 * w1
    u_out[...] = raw1[...] / b2


VM = pl.BlockSpec(memory_space=pltpu.VMEM)
SM = pl.BlockSpec(memory_space=pltpu.SMEM)
HBM = pl.BlockSpec(memory_space=pltpu.HBM)


def call(kernel, outs, args, specs=None, scratch=(), limit=32):
    return pl.pallas_call(
        kernel,
        out_shape=[jax.ShapeDtypeStruct(shape, kind) for shape, kind in outs],
        in_specs=specs or [SM] + [VM] * (len(args) - 1),
        out_specs=[VM] * len(outs),
        scratch_shapes=[pltpu.VMEM(s, F32) if isinstance(s, tuple) else s for s in scratch],
        compiler_params=pltpu.CompilerParams(vmem_limit_bytes=limit * 2**20),
        name=kernel.__name__,
    )(*args)


def shards(data, blocks, block_cols, block_rows, block_counts, reg_weight):
    pos = jnp.stack([lax.axis_index("ray"), lax.axis_index("tile")]).astype(jnp.int32)
    weight = reg_weight.reshape(CELLS, LANES)
    message = ((RAY, MSG, LANES), BF16)
    tile_message = ((TILE, TMSG, LANES), BF16)
    scalar = ((1, LANES), F32)
    cells = ((CELLS, LANES), F32)
    rays = ((KB, LANES), F32)
    slab = ((XS, CY, LANES), F32)
    edges = (2, 8, LANES)
    slabs = [(XS + 2, CY, LANES), (TILE, 8, LANES)]
    own = jnp.concatenate([data.reshape(KOWN, LANES), weight], axis=0)
    start = lax.all_to_all(jnp.broadcast_to(own, (TILE,) + own.shape), "tile", 0, 0)
    p_hot, p_wide, r_hot, r_turned, note = call(
        kernel_index,
        [
            ((RAY * CAP, SLOTS), BF16),
            ((SLOTS, RAY * MSG), BF16),
            ((KB, SLOTS), BF16),
            ((SLOTS, KB), BF16),
            ((RAY * CAP, LANES), F32),
        ],
        (block_cols[0], block_rows[0], block_counts),
        [VM] * 3,
    )
    send, values = call(
        kernel_start,
        [message, ((SLOTS, LANES, LANES), BF16)],
        (pos, start, note, blocks[0, 0], p_hot, r_turned),
        [SM, VM, VM, HBM, VM, VM],
        [pltpu.SemaphoreType.DMA((CHUNKS,))],
        48,
    )
    recv = lax.all_to_all(send, "ray", 0, 0)
    send, v0_raw, q_hot, beta0 = call(
        kernel_first_v,
        [message, cells, ((RAY * CAP, CELLS), BF16), scalar],
        (pos, recv),
        scratch=[edges],
    )
    recv = lax.all_to_all(send, "ray", 0, 0)
    (send,) = call(
        kernel_forward, [tile_message], (pos, recv, p_wide, r_hot, values, v0_raw), scratch=[(16, LANES)]
    )
    recv = lax.all_to_all(send, "tile", 0, 0)
    send, raw1, raw2, alpha0, nq = call(
        kernel_back,
        [message, rays, slab, scalar, cells],
        (pos, recv, v0_raw, start, beta0, values, p_hot, r_turned),
        scratch=[edges] + slabs + slabs[:1],
    )
    recv = lax.all_to_all(send, "ray", 0, 0)
    send, v1_raw, beta1 = call(
        kernel_next_v,
        [message, cells, scalar],
        (pos, recv, q_hot, v0_raw, alpha0, nq),
        scratch=[edges],
    )
    recv = lax.all_to_all(send, "ray", 0, 0)
    (send,) = call(
        kernel_forward, [tile_message], (pos, recv, p_wide, r_hot, values, v1_raw), scratch=[(16, LANES)]
    )
    recv = lax.all_to_all(send, "tile", 0, 0)
    send, raw1_own, alpha1 = call(
        kernel_last_norm,
        [((RAY, 1, LANES), F32), ((KOWN, LANES), F32), scalar],
        (pos, recv, v1_raw, start, beta1, raw1, raw2),
        scratch=[(TILE, KOWN, LANES)] + slabs,
    )
    recv = lax.all_to_all(send, "ray", 0, 0)
    model, rays = call(
        kernel_end,
        [cells, ((KOWN, LANES), F32)],
        (recv, v0_raw, v1_raw, raw1_own, beta0, beta1, alpha0, alpha1),
        [VM] * 8,
    )
    return model.reshape(reg_weight.shape), rays.reshape(data.shape)


def solution(mesh):
    return jax.shard_map(
        shards,
        mesh=mesh,
        in_specs=(
            P(("ray", "tile")),
            P("ray", "tile", None, None, None),
            P("ray", "tile", None),
            P("ray", "tile", None),
            P("ray", "tile"),
            P("tile", "ray", None),
        ),
        out_specs=(P("tile", "ray", None), P(("ray", "tile"))),
        check_vma=False,
    )
```

```python
import jax
import jax.numpy as jnp
from jax import lax
from jax.experimental import pallas as pl
from jax.experimental.pallas import tpu as pltpu
from jax.sharding import PartitionSpec as P

RAY = 32
TILE = 8
CAP = 8
CX = 4
CY = 8
CELLS = CX * CY
SLOTS = 128
LANES = 128
KB = 64
KOWN = KB // TILE
MSG = 2 * CAP
TMSG = KB + CELLS + 16
SMSG = KOWN + CELLS
HALF = SLOTS // 2
CHUNKS = 2
XS = TILE * CX
eps = 1e-06

F32 = jnp.float32
BF16 = jnp.bfloat16


def iota(shape, dim):
    return lax.broadcasted_iota(jnp.int32, shape, dim)


def dot(a, b, ca, cb):
    return lax.dot_general(a, b, (((ca,), (cb,)), ((), ())), preferred_element_type=F32)


def onehot_dot(hot, x, ca, cb):
    high = x.astype(BF16)
    rest = x - high.astype(F32)
    mid = rest.astype(BF16)
    low = (rest - mid.astype(F32)).astype(BF16)
    return dot(hot, high, ca, cb) + (dot(hot, mid, ca, cb) + dot(hot, low, ca, cb))


def total(x):
    return jnp.sum(jnp.sum(x, axis=0, keepdims=True), axis=1, keepdims=True)


def terms(x):
    high = x.astype(BF16).astype(F32)
    mid = (x - high).astype(BF16).astype(F32)
    return high, mid, x - high - mid


def wide(x):
    return jnp.broadcast_to(x, (1, LANES))


def lane_sides(f):
    lane = iota(f.shape, 1)
    left = jnp.where(lane == 0, 0.0, pltpu.roll(f, 1, 1))
    right = jnp.where(lane == LANES - 1, 0.0, pltpu.roll(f, LANES - 1, 1))
    return left + right


def row_sides(f, low, high):
    row = iota(f.shape, 0)
    below = jnp.where(row == 0, low, pltpu.roll(f, 1, 0))
    above = jnp.where(row == CY - 1, high, pltpu.roll(f, CY - 1, 0))
    return below + above


def eight(pair, at):
    first, second = pair
    return first[at : at + 8] if at < HALF else second[at - HALF : at - HALF + 8]


def bring(blocks, start, held, sems):
    per = HALF // CHUNKS
    copies = [
        pltpu.make_async_copy(blocks.at[pl.ds(start + c * per, per)], held.at[pl.ds(c * per, per)], sems.at[c])
        for c in range(CHUNKS)
    ]
    for copy in copies:
        copy.start()
    return copies


def products_t(picked, pair, start, stop):
    row = iota((8, LANES), 0)
    out = []
    for at in range(start, stop, 8):
        p = picked[at : at + 8, :]
        lhs = jnp.concatenate([jnp.where(row == i, p, 0.0) for i in range(8)], axis=1)
        out.append(dot(lhs.astype(BF16), eight(pair, at).reshape(8 * LANES, LANES), 1, 0))
    return out


def products(x, pair, r_hot):
    row = iota((8, LANES), 0)
    out = []
    for q in range(SLOTS // 8):
        p = x[8 * q : 8 * q + 8, :]
        lhs = jnp.concatenate([jnp.where(row == i, p, 0.0) for i in range(8)], axis=1)
        some = eight(pair, 8 * q)
        rhs = jnp.concatenate([some[i] for i in range(8)], axis=1)
        out.append(dot(lhs.astype(BF16), rhs, 1, 1))
    return onehot_dot(r_hot, jnp.concatenate(out, axis=0), 1, 0)


def edge_tiles(scratch, low, high, scalar):
    for x in range(CX):
        scratch[0, x : x + 1, :] = low[x]
        scratch[1, x : x + 1, :] = high[x]
    for i, term in enumerate(terms(scalar)):
        scratch[0, CX + i : CX + i + 1, :] = wide(term)
        scratch[1, CX + i : CX + i + 1, :] = wide(term)
    scratch[0, 7:8, :] = jnp.zeros((1, LANES), F32)
    scratch[1, 7:8, :] = jnp.zeros((1, LANES), F32)
    return scratch[0], scratch[1]


def kernel_index(cols, rows, count, blocks, p_out, p_wide_out, r_out, r_turned_out, note_out, first_out, sems):
    copies = bring(blocks, 0, first_out, sems)
    col = cols[...]
    live = iota((1, SLOTS), 1) < count[...]
    slab = RAY * CY
    owner = lax.div(lax.rem(col, slab), CY)
    local = lax.div(col, slab) * CY + lax.rem(col, CY)
    own_hot = iota((RAY, SLOTS), 0) == owner
    before = (iota((SLOTS, SLOTS), 0) < iota((SLOTS, SLOTS), 1)).astype(F32).astype(BF16)
    earlier = dot(own_hot.astype(F32).astype(BF16), before, 1, 0)
    rank = jnp.sum(jnp.where(own_hot, earlier, 0.0), axis=0, keepdims=True).astype(jnp.int32)
    p_f = ((iota((RAY * CAP, SLOTS), 0) == owner * CAP + rank) & live).astype(F32)
    p_out[...] = p_f.astype(BF16)
    p_wide = ((iota((RAY * MSG, SLOTS), 0) == owner * MSG + rank) & live).astype(F32)
    p_wide_out[...] = p_wide.T.astype(BF16)
    r_f = ((iota((KB, SLOTS), 0) == rows[...]) & live).astype(F32)
    r_out[...] = r_f.astype(BF16)
    r_turned_out[...] = r_f.T.astype(BF16)
    ids = jnp.sum(p_f * (local + 1).astype(F32), axis=1, keepdims=True) - 1.0
    note_out[...] = jnp.broadcast_to(ids, (RAY * CAP, LANES))
    for copy in copies:
        copy.wait()


def send_contributions(send, p_hot, contrib, notes):
    slots = dot(p_hot, contrib.astype(BF16), 1, 0)
    for d in range(RAY):
        send[d] = jnp.concatenate([slots[CAP * d : CAP * d + CAP], notes(d)], axis=0).astype(BF16)


def received(recv):
    both = [recv[d].astype(F32) for d in range(RAY)]
    contrib = jnp.concatenate([x[0:CAP] for x in both], axis=0).astype(BF16)
    return contrib, [x[CAP:MSG] for x in both]


def kernel_start(pos_ref, start, note, blocks, first, p_hot, r_turned, send, second_out, sems):
    copies = bring(blocks, HALF, second_out, sems)
    data = start[:, 0:KOWN, :].reshape(KB, LANES)
    picked = dot(r_turned[...], data.astype(BF16), 1, 0)
    pair = (first, second_out)
    contrib = products_t(picked, pair, 0, HALF)
    per = HALF // CHUNKS
    for c, copy in enumerate(copies):
        copy.wait()
        contrib += products_t(picked, pair, HALF + c * per, HALF + (c + 1) * per)
    contrib = jnp.concatenate(contrib, axis=0)
    quarter = iota((CAP, LANES), 1) // CELLS
    high, mid, low = terms(total(data * data))
    squares = jnp.where(quarter == 1, high, jnp.where(quarter == 2, mid, low))
    send_contributions(
        send, p_hot[...], contrib,
        lambda d: jnp.where(quarter == 0, note[CAP * d : CAP * d + CAP, :], squares),
    )


def send_columns(send, q_hot, v_raw, scratch, low, high, scalar, ray):
    columns = dot(q_hot, v_raw.astype(BF16), 1, 0)
    low, high = edge_tiles(scratch, low, high, scalar)
    for d in range(RAY):
        edge = jnp.where(d > ray, high, low)
        send[d] = jnp.concatenate([columns[CAP * d : CAP * d + CAP], edge], axis=0).astype(BF16)


def kernel_first_v(pos_ref, recv, send, v_out, q_out, beta_out, scratch):
    contrib, notes = received(recv)
    norm = notes[0][0:1]
    for d in range(1, RAY):
        norm = norm + notes[d][0:1]
    note = jnp.concatenate(notes, axis=0)
    q_hot = (note[:, 0:CELLS] == iota((RAY * CAP, CELLS), 1).astype(F32)).astype(F32).astype(BF16)
    q_out[...] = q_hot
    lane = iota((1, LANES), 1)
    squares = total(jnp.where((lane > 0) & (lane % CELLS == 0), norm, 0.0))
    beta = jnp.sqrt(squares + eps)
    beta_out[...] = wide(beta)
    v_raw = dot(q_hot, contrib, 0, 0) / beta
    v_out[...] = v_raw
    low = [v_raw[CY * x : CY * x + 1, :] for x in range(CX)]
    high = [v_raw[CY * x + CY - 1 : CY * x + CY, :] for x in range(CX)]
    send_columns(send, q_hot, v_raw, scratch, low, high, total(v_raw * v_raw), pos_ref[0])


def kernel_forward(pos_ref, recv, p_wide, r_hot, first, second, v_raw, send, scratch):
    ray = pos_ref[0]
    x = dot(p_wide[...], recv[...].reshape(RAY * MSG, LANES), 1, 0)
    part = products(x, (first, second), r_hot[...]).astype(BF16)
    norm = jnp.zeros((MSG, LANES), F32)
    for d in range(RAY):
        norm = norm + recv[d].astype(F32)
    low = recv[jnp.maximum(ray - 1, 0)].astype(F32)
    high = recv[jnp.minimum(ray + 1, RAY - 1)].astype(F32)
    scratch[0:CX, :] = jnp.where(ray > 0, low[CAP : CAP + CX], 0.0)
    scratch[CX : 2 * CX, :] = jnp.where(ray < RAY - 1, high[CAP : CAP + CX], 0.0)
    at = CAP + CX
    norm = norm[at : at + 1] + (norm[at + 1 : at + 2] + norm[at + 2 : at + 3])
    for i, term in enumerate(terms(norm)):
        scratch[2 * CX + i : 2 * CX + i + 1, :] = term
    scratch[2 * CX + 3 : 16, :] = jnp.zeros((16 - 2 * CX - 3, LANES), F32)
    edge = scratch[...].astype(BF16)
    mine = v_raw[...].astype(BF16)
    for t in range(TILE):
        send[t, 0:KB, :] = part
        send[t, KB : KB + CELLS, :] = mine
        send[t, KB + CELLS : TMSG, :] = edge


def gathered(recv, v_raw, tile, slab, edges):
    kv = recv[0, 0:KB, :].astype(F32)
    for t in range(1, TILE):
        kv = kv + recv[t, 0:KB, :].astype(F32)
    slab[0] = jnp.zeros((CY, LANES), F32)
    slab[XS + 1] = jnp.zeros((CY, LANES), F32)
    norm = jnp.zeros((8, LANES), F32)
    for t in range(TILE):
        for h in range(CELLS // 16):
            both = recv[t, KB + 16 * h : KB + 16 * h + 16, :].astype(F32)
            slab[CX * t + 2 * h + 1] = both[0:CY]
            slab[CX * t + 2 * h + 2] = both[CY : 2 * CY]
        edge = recv[t, KB + CELLS : TMSG, :].astype(F32)
        edges[t] = edge[0:8]
        norm = norm + edge[8:16]
    for x in range(CX):
        slab[CX * tile + x + 1] = v_raw[CY * x : CY * x + CY, :]
    return kv, jnp.sqrt(norm[0:1] + (norm[1:2] + norm[2:3]) + eps)


def slab_laplace(slab, edges, index):
    t, x = divmod(index, CX)
    f = slab[index + 1]
    beside = row_sides(f, edges[t, x : x + 1, :], edges[t, CX + x : CX + x + 1, :])
    beside = beside + lane_sides(f) + slab[index] + slab[index + 2]
    return 6.0 * f - beside


def cell_weight(start, index):
    t, x = divmod(index, CX)
    return start[t, KOWN + CY * x : KOWN + CY * x + CY, :]


def kernel_back(
    pos_ref, recv, v_raw, start, beta0, first, second, p_hot, r_turned,
    send, raw1_out, raw2_out, alpha_out, nq_out,
    scratch, slab, edges, field,
):
    ray, tile = pos_ref[0], pos_ref[1]
    kv, alpha = gathered(recv, v_raw, tile, slab, edges)
    alpha_out[...] = alpha
    raw1 = kv / alpha - alpha * (start[:, 0:KOWN, :].reshape(KB, LANES) / beta0[...])
    raw1_out[...] = raw1
    field[0] = jnp.zeros((CY, LANES), F32)
    field[XS + 1] = jnp.zeros((CY, LANES), F32)
    squares = jnp.zeros((CY, LANES), F32)
    for i in range(XS):
        weight = cell_weight(start, i)
        raw2 = weight * (slab_laplace(slab, edges, i) / alpha)
        raw2_out[i] = raw2
        squares = squares + raw2 * raw2
        field[i + 1] = weight * raw2
    picked = dot(r_turned[...], raw1.astype(BF16), 1, 0)
    contrib = jnp.concatenate(products_t(picked, (first, second), 0, SLOTS), axis=0)
    low, high = [], []
    for x in range(CX):
        at = tile * CX + x + 1
        f = field[at]
        beside = row_sides(f, 0.0, 0.0) + lane_sides(f) + field[at - 1] + field[at + 1]
        nq_out[CY * x : CY * x + CY, :] = 6.0 * f - beside
        low.append(f[0:1])
        high.append(f[CY - 1 : CY])
    low, high = edge_tiles(scratch, low, high, total(raw1 * raw1) + total(squares))
    send_contributions(send, p_hot[...], contrib, lambda d: jnp.where(d > ray, high, low))


def kernel_next_v(pos_ref, recv, q_ref, v0_raw, alpha0, nq, send, v_out, beta_out, scratch):
    ray = pos_ref[0]
    contrib, notes = received(recv)
    q_hot = q_ref[...]
    norm = notes[0]
    for d in range(1, RAY):
        norm = norm + notes[d]
    beta = jnp.sqrt(norm[CX : CX + 1] + (norm[CX + 1 : CX + 2] + norm[CX + 2 : CX + 3]) + eps)
    beta_out[...] = beta
    z = dot(q_hot, contrib, 0, 0)
    low = jnp.where(ray > 0, recv[jnp.maximum(ray - 1, 0)].astype(F32)[CAP:MSG], 0.0)
    high = jnp.where(ray < RAY - 1, recv[jnp.minimum(ray + 1, RAY - 1)].astype(F32)[CAP:MSG], 0.0)
    row = iota((CY, LANES), 0)
    squares = jnp.zeros((CY, LANES), F32)
    edges_low, edges_high, parts = [], [], []
    for x in range(CX):
        cut = slice(CY * x, CY * x + CY)
        edge = jnp.where(row == 0, low[x : x + 1], 0.0) + jnp.where(row == CY - 1, high[x : x + 1], 0.0)
        v_raw = (z[cut] + (nq[cut, :] - edge)) / beta - beta * (v0_raw[cut, :] / alpha0[...])
        v_out[cut, :] = v_raw
        parts.append(v_raw)
        squares = squares + v_raw * v_raw
        edges_low.append(v_raw[0:1])
        edges_high.append(v_raw[CY - 1 : CY])
    send_columns(send, q_hot, jnp.concatenate(parts, axis=0), scratch, edges_low, edges_high, total(squares), ray)


def kernel_last_norm(
    pos_ref, recv, v_raw, start, beta1, raw1_ref, raw2_ref, send, raw1_out, alpha_out, scratch, slab, edges
):
    tile = pos_ref[1]
    kv, alpha = gathered(recv, v_raw, tile, slab, edges)
    alpha_out[...] = alpha
    raw1 = kv / alpha - alpha * (raw1_ref[...] / beta1[...])
    scratch[...] = raw1.reshape(TILE, KOWN, LANES)
    raw1_out[...] = scratch[tile]
    squares = jnp.zeros((CY, LANES), F32)
    for i in range(XS):
        raw2 = cell_weight(start, i) * (slab_laplace(slab, edges, i) / alpha) - alpha * (raw2_ref[i] / beta1[...])
        squares = squares + raw2 * raw2
    norm = total(raw1 * raw1) + total(squares)
    send[...] = jnp.broadcast_to(norm.reshape(1, 1, 1), (RAY, 1, LANES))


def kernel_end(recv, v0_raw, v1_raw, raw1, beta0, beta1, alpha0, alpha1, model_out, u_out):
    norm = recv[0]
    for d in range(1, RAY):
        norm = norm + recv[d]
    b0, b1, b2 = beta0[...], beta1[...], jnp.sqrt(norm + eps)
    a0, a1 = alpha0[...], alpha1[...]
    v0, v1 = v0_raw[...] / a0, v1_raw[...] / a1
    rho1 = jnp.sqrt(a0 * a0 + b1 * b1)
    cosine1, sine1 = a0 / rho1, b1 / rho1
    theta = sine1 * a1
    rhobar = -cosine1 * a1
    phi1, phibar = cosine1 * b0, sine1 * b0
    w1 = v1 - theta / rho1 * v0
    rho2 = jnp.sqrt(rhobar * rhobar + b2 * b2)
    phi2 = rhobar / rho2 * phibar
    model_out[...] = phi1 / rho1 * v0 + phi2 / rho2 * w1
    u_out[...] = raw1[...] / b2


VM = pl.BlockSpec(memory_space=pltpu.VMEM)
SM = pl.BlockSpec(memory_space=pltpu.SMEM)
HBM = pl.BlockSpec(memory_space=pltpu.HBM)


def call(kernel, outs, args, specs=None, scratch=(), limit=32):
    return pl.pallas_call(
        kernel,
        out_shape=[jax.ShapeDtypeStruct(shape, kind) for shape, kind in outs],
        in_specs=specs or [SM] + [VM] * (len(args) - 1),
        out_specs=[VM] * len(outs),
        scratch_shapes=[pltpu.VMEM(s, F32) if isinstance(s, tuple) else s for s in scratch],
        compiler_params=pltpu.CompilerParams(vmem_limit_bytes=limit * 2**20),
        name=kernel.__name__,
    )(*args)


def shards(data, blocks, block_cols, block_rows, block_counts, reg_weight):
    pos = jnp.stack([lax.axis_index("ray"), lax.axis_index("tile")]).astype(jnp.int32)
    weight = reg_weight.reshape(CELLS, LANES)
    message = ((RAY, MSG, LANES), BF16)
    tile_message = ((TILE, TMSG, LANES), BF16)
    scalar = ((1, LANES), F32)
    cells = ((CELLS, LANES), F32)
    rays = ((KB, LANES), F32)
    slab = ((XS, CY, LANES), F32)
    edges = (2, 8, LANES)
    slabs = [(XS + 2, CY, LANES), (TILE, 8, LANES)]
    own = jnp.concatenate([data.reshape(KOWN, LANES), weight], axis=0)
    start = lax.all_to_all(jnp.broadcast_to(own, (TILE,) + own.shape), "tile", 0, 0)
    half = ((HALF, LANES, LANES), BF16)
    p_hot, p_wide, r_hot, r_turned, note, first = call(
        kernel_index,
        [
            ((RAY * CAP, SLOTS), BF16),
            ((SLOTS, RAY * MSG), BF16),
            ((KB, SLOTS), BF16),
            ((SLOTS, KB), BF16),
            ((RAY * CAP, LANES), F32),
            half,
        ],
        (block_cols[0], block_rows[0], block_counts, blocks[0, 0]),
        [VM] * 3 + [HBM],
        [pltpu.SemaphoreType.DMA((CHUNKS,))],
        50,
    )
    send, second = call(
        kernel_start,
        [message, half],
        (pos, start, note, blocks[0, 0], first, p_hot, r_turned),
        [SM, VM, VM, HBM, VM, VM, VM],
        [pltpu.SemaphoreType.DMA((CHUNKS,))],
        48,
    )
    recv = lax.all_to_all(send, "ray", 0, 0)
    send, v0_raw, q_hot, beta0 = call(
        kernel_first_v,
        [message, cells, ((RAY * CAP, CELLS), BF16), scalar],
        (pos, recv),
        scratch=[edges],
    )
    recv = lax.all_to_all(send, "ray", 0, 0)
    (send,) = call(
        kernel_forward, [tile_message], (pos, recv, p_wide, r_hot, first, second, v0_raw), scratch=[(16, LANES)]
    )
    recv = lax.all_to_all(send, "tile", 0, 0)
    send, raw1, raw2, alpha0, nq = call(
        kernel_back,
        [message, rays, slab, scalar, cells],
        (pos, recv, v0_raw, start, beta0, first, second, p_hot, r_turned),
        scratch=[edges] + slabs + slabs[:1],
    )
    recv = lax.all_to_all(send, "ray", 0, 0)
    send, v1_raw, beta1 = call(
        kernel_next_v,
        [message, cells, scalar],
        (pos, recv, q_hot, v0_raw, alpha0, nq),
        scratch=[edges],
    )
    recv = lax.all_to_all(send, "ray", 0, 0)
    (send,) = call(
        kernel_forward, [tile_message], (pos, recv, p_wide, r_hot, first, second, v1_raw), scratch=[(16, LANES)]
    )
    recv = lax.all_to_all(send, "tile", 0, 0)
    send, raw1_own, alpha1 = call(
        kernel_last_norm,
        [((RAY, 1, LANES), F32), ((KOWN, LANES), F32), scalar],
        (pos, recv, v1_raw, start, beta1, raw1, raw2),
        scratch=[(TILE, KOWN, LANES)] + slabs,
    )
    recv = lax.all_to_all(send, "ray", 0, 0)
    model, rays = call(
        kernel_end,
        [cells, ((KOWN, LANES), F32)],
        (recv, v0_raw, v1_raw, raw1_own, beta0, beta1, alpha0, alpha1),
        [VM] * 8,
    )
    return model.reshape(reg_weight.shape), rays.reshape(data.shape)


def solution(mesh):
    return jax.shard_map(
        shards,
        mesh=mesh,
        in_specs=(
            P(("ray", "tile")),
            P("ray", "tile", None, None, None),
            P("ray", "tile", None),
            P("ray", "tile", None),
            P("ray", "tile"),
            P("tile", "ray", None),
        ),
        out_specs=(P("tile", "ray", None), P(("ray", "tile"))),
        check_vma=False,
    )
```

```python
import functools

import jax
import jax.numpy as jnp
from jax import lax
from jax.experimental import pallas as pl
from jax.experimental.pallas import tpu as pltpu
from jax.sharding import PartitionSpec as P

RAY = 32
TILE = 8
CAP = 8
CX = 4
CY = 8
CELLS = CX * CY
SLOTS = 128
LANES = 128
KB = 64
KOWN = KB // TILE
MSG = 2 * CAP
TMSG = KB + CELLS + 16
SMSG = KOWN + CELLS
HALF = SLOTS // 2
CHUNKS = 2
XS = TILE * CX
eps = 1e-06

F32 = jnp.float32
BF16 = jnp.bfloat16


def iota(shape, dim):
    return lax.broadcasted_iota(jnp.int32, shape, dim)


def dot(a, b, ca, cb):
    return lax.dot_general(a, b, (((ca,), (cb,)), ((), ())), preferred_element_type=F32)


def onehot_dot(hot, x, ca, cb):
    high = x.astype(BF16)
    rest = x - high.astype(F32)
    mid = rest.astype(BF16)
    low = (rest - mid.astype(F32)).astype(BF16)
    return dot(hot, high, ca, cb) + (dot(hot, mid, ca, cb) + dot(hot, low, ca, cb))


def total(x):
    return jnp.sum(jnp.sum(x, axis=0, keepdims=True), axis=1, keepdims=True)


def terms(x):
    high = x.astype(BF16).astype(F32)
    mid = (x - high).astype(BF16).astype(F32)
    return high, mid, x - high - mid


def wide(x):
    return jnp.broadcast_to(x, (1, LANES))


def lane_sides(f):
    lane = iota(f.shape, 1)
    left = jnp.where(lane == 0, 0.0, pltpu.roll(f, 1, 1))
    right = jnp.where(lane == LANES - 1, 0.0, pltpu.roll(f, LANES - 1, 1))
    return left + right


def row_sides(f, low, high):
    row = iota(f.shape, 0)
    below = jnp.where(row == 0, low, pltpu.roll(f, 1, 0))
    above = jnp.where(row == CY - 1, high, pltpu.roll(f, CY - 1, 0))
    return below + above


def eight(pair, at):
    first, second = pair
    return first[at : at + 8] if at < HALF else second[at - HALF : at - HALF + 8]


def bring(blocks, start, held, sems):
    per = HALF // CHUNKS
    copies = [
        pltpu.make_async_copy(blocks.at[pl.ds(start + c * per, per)], held.at[pl.ds(c * per, per)], sems.at[c])
        for c in range(CHUNKS)
    ]
    for copy in copies:
        copy.start()
    return copies


def products_t(picked, pair, start, stop):
    row = iota((8, LANES), 0)
    out = []
    for at in range(start, stop, 8):
        p = picked[at : at + 8, :]
        lhs = jnp.concatenate([jnp.where(row == i, p, 0.0) for i in range(8)], axis=1)
        out.append(dot(lhs.astype(BF16), eight(pair, at).reshape(8 * LANES, LANES), 1, 0))
    return out


def products(parts, pair, r_hot):
    row = iota((8, LANES), 0)
    out = []
    for q in range(SLOTS // 8):
        lhs = [
            jnp.concatenate([jnp.where(row == i, x[8 * q : 8 * q + 8, :], 0.0) for i in range(8)], axis=1)
            for x in parts
        ]
        some = eight(pair, 8 * q)
        rhs = jnp.concatenate([some[i] for i in range(8)], axis=1)
        both = dot(jnp.concatenate(lhs, axis=0).astype(BF16), rhs, 1, 1)
        out.append(both[0:8] + both[8:16] if len(parts) == 2 else both)
    return onehot_dot(r_hot, jnp.concatenate(out, axis=0), 1, 0)


def edge_tiles(scratch, low, high, scalar):
    for x in range(CX):
        scratch[0, x : x + 1, :] = low[x]
        scratch[1, x : x + 1, :] = high[x]
    for i, term in enumerate(terms(scalar)):
        scratch[0, CX + i : CX + i + 1, :] = wide(term)
        scratch[1, CX + i : CX + i + 1, :] = wide(term)
    scratch[0, 7:8, :] = jnp.zeros((1, LANES), F32)
    scratch[1, 7:8, :] = jnp.zeros((1, LANES), F32)
    return scratch[0], scratch[1]


def kernel_index(cols, rows, count, blocks, p_out, p_wide_out, r_out, r_turned_out, note_out, first_out, sems):
    copies = bring(blocks, 0, first_out, sems)
    col = cols[...]
    live = iota((1, SLOTS), 1) < count[...]
    slab = RAY * CY
    owner = lax.div(lax.rem(col, slab), CY)
    local = lax.div(col, slab) * CY + lax.rem(col, CY)
    own_hot = iota((RAY, SLOTS), 0) == owner
    before = (iota((SLOTS, SLOTS), 0) < iota((SLOTS, SLOTS), 1)).astype(F32).astype(BF16)
    earlier = dot(own_hot.astype(F32).astype(BF16), before, 1, 0)
    rank = jnp.sum(jnp.where(own_hot, earlier, 0.0), axis=0, keepdims=True).astype(jnp.int32)
    p_f = ((iota((RAY * CAP, SLOTS), 0) == owner * CAP + rank) & live).astype(F32)
    p_out[...] = p_f.astype(BF16)
    p_wide = ((iota((RAY * MSG, SLOTS), 0) == owner * MSG + rank) & live).astype(F32)
    p_wide_out[...] = p_wide.T.astype(BF16)
    r_f = ((iota((KB, SLOTS), 0) == rows[...]) & live).astype(F32)
    r_out[...] = r_f.astype(BF16)
    r_turned_out[...] = r_f.T.astype(BF16)
    ids = jnp.sum(p_f * (local + 1).astype(F32), axis=1, keepdims=True) - 1.0
    note_out[...] = jnp.broadcast_to(ids, (RAY * CAP, LANES))
    for copy in copies:
        copy.wait()


def send_contributions(send, p_hot, contrib, notes):
    slots = dot(p_hot, contrib.astype(BF16), 1, 0)
    for d in range(RAY):
        send[d] = jnp.concatenate([slots[CAP * d : CAP * d + CAP], notes(d)], axis=0).astype(BF16)


def received(recv):
    both = [recv[d].astype(F32) for d in range(RAY)]
    contrib = jnp.concatenate([x[0:CAP] for x in both], axis=0).astype(BF16)
    return contrib, [x[CAP:MSG] for x in both]


def kernel_start(pos_ref, start, note, blocks, first, p_hot, r_turned, send, second_out, sems):
    copies = bring(blocks, HALF, second_out, sems)
    data = start[:, 0:KOWN, :].reshape(KB, LANES)
    picked = dot(r_turned[...], data.astype(BF16), 1, 0)
    pair = (first, second_out)
    contrib = products_t(picked, pair, 0, HALF)
    per = HALF // CHUNKS
    for c, copy in enumerate(copies):
        copy.wait()
        contrib += products_t(picked, pair, HALF + c * per, HALF + (c + 1) * per)
    contrib = jnp.concatenate(contrib, axis=0)
    quarter = iota((CAP, LANES), 1) // CELLS
    high, mid, low = terms(total(data * data))
    squares = jnp.where(quarter == 1, high, jnp.where(quarter == 2, mid, low))
    send_contributions(
        send, p_hot[...], contrib,
        lambda d: jnp.where(quarter == 0, note[CAP * d : CAP * d + CAP, :], squares),
    )


def send_columns(send, q_hot, v_raw, scratch, low, high, scalar, ray):
    columns = onehot_dot(q_hot, v_raw, 1, 0)
    low, high = edge_tiles(scratch, low, high, scalar)
    for d in range(RAY):
        edge = jnp.where(d > ray, high, low)
        send[d] = jnp.concatenate([columns[CAP * d : CAP * d + CAP], edge], axis=0).astype(send.dtype)


def kernel_first_v(pos_ref, recv, send, v_out, q_out, beta_out, scratch):
    contrib, notes = received(recv)
    norm = notes[0][0:1]
    for d in range(1, RAY):
        norm = norm + notes[d][0:1]
    note = jnp.concatenate(notes, axis=0)
    q_hot = (note[:, 0:CELLS] == iota((RAY * CAP, CELLS), 1).astype(F32)).astype(F32).astype(BF16)
    q_out[...] = q_hot
    lane = iota((1, LANES), 1)
    squares = total(jnp.where((lane > 0) & (lane % CELLS == 0), norm, 0.0))
    beta = jnp.sqrt(squares + eps)
    beta_out[...] = wide(beta)
    v_raw = dot(q_hot, contrib, 0, 0) / beta
    v_out[...] = v_raw
    low = [v_raw[CY * x : CY * x + 1, :] for x in range(CX)]
    high = [v_raw[CY * x + CY - 1 : CY * x + CY, :] for x in range(CX)]
    send_columns(send, q_hot, v_raw, scratch, low, high, total(v_raw * v_raw), pos_ref[0])


def kernel_forward(pos_ref, recv, p_wide, r_hot, first, second, v_raw, send, scratch, *, last):
    ray = pos_ref[0]
    asked = recv[...].reshape(RAY * MSG, LANES)
    parts = [asked.astype(BF16)]
    if last:
        parts.append((asked - parts[0].astype(F32)).astype(BF16))
    full = products([dot(p_wide[...], x, 1, 0) for x in parts], (first, second), r_hot[...])
    part = full.astype(BF16)
    rest = full - part.astype(F32)
    norm = jnp.zeros((MSG, LANES), F32)
    for d in range(RAY):
        norm = norm + recv[d].astype(F32)
    low = recv[jnp.maximum(ray - 1, 0)].astype(F32)
    high = recv[jnp.minimum(ray + 1, RAY - 1)].astype(F32)
    scratch[0:CX, :] = jnp.where(ray > 0, low[CAP : CAP + CX], 0.0)
    scratch[CX : 2 * CX, :] = jnp.where(ray < RAY - 1, high[CAP : CAP + CX], 0.0)
    at = CAP + CX
    norm = norm[at : at + 1] + (norm[at + 1 : at + 2] + norm[at + 2 : at + 3])
    for i, term in enumerate(terms(norm)):
        scratch[2 * CX + i : 2 * CX + i + 1, :] = term
    scratch[2 * CX + 3 : 16, :] = jnp.zeros((16 - 2 * CX - 3, LANES), F32)
    edge = scratch[...].astype(BF16)
    mine = v_raw[...].astype(BF16)
    for t in range(TILE):
        send[t, 0:KB, :] = part
        send[t, KB : KB + CELLS, :] = mine
        send[t, KB + CELLS : TMSG, :] = edge
        if last:
            own = rest[KOWN * t : KOWN * t + KOWN]
            send[t, TMSG : TMSG + 16, :] = jnp.concatenate([own, jnp.zeros_like(own)], axis=0).astype(BF16)


def gathered(recv, v_raw, tile, slab, edges):
    kv = recv[0, 0:KB, :].astype(F32)
    for t in range(1, TILE):
        kv = kv + recv[t, 0:KB, :].astype(F32)
    slab[0] = jnp.zeros((CY, LANES), F32)
    slab[XS + 1] = jnp.zeros((CY, LANES), F32)
    norm = jnp.zeros((8, LANES), F32)
    for t in range(TILE):
        for h in range(CELLS // 16):
            both = recv[t, KB + 16 * h : KB + 16 * h + 16, :].astype(F32)
            slab[CX * t + 2 * h + 1] = both[0:CY]
            slab[CX * t + 2 * h + 2] = both[CY : 2 * CY]
        edge = recv[t, KB + CELLS : TMSG, :].astype(F32)
        edges[t] = edge[0:8]
        norm = norm + edge[8:16]
    for x in range(CX):
        slab[CX * tile + x + 1] = v_raw[CY * x : CY * x + CY, :]
    return kv, jnp.sqrt(norm[0:1] + (norm[1:2] + norm[2:3]) + eps)


def slab_laplace(slab, edges, index):
    t, x = divmod(index, CX)
    f = slab[index + 1]
    beside = row_sides(f, edges[t, x : x + 1, :], edges[t, CX + x : CX + x + 1, :])
    beside = beside + lane_sides(f) + slab[index] + slab[index + 2]
    return 6.0 * f - beside


def cell_weight(start, index):
    t, x = divmod(index, CX)
    return start[t, KOWN + CY * x : KOWN + CY * x + CY, :]


def kernel_back(
    pos_ref, recv, v_raw, start, beta0, first, second, p_hot, r_turned,
    send, raw1_out, raw2_out, alpha_out, nq_out,
    scratch, slab, edges, field,
):
    ray, tile = pos_ref[0], pos_ref[1]
    kv, alpha = gathered(recv, v_raw, tile, slab, edges)
    alpha_out[...] = alpha
    raw1 = kv / alpha - alpha * (start[:, 0:KOWN, :].reshape(KB, LANES) / beta0[...])
    raw1_out[...] = raw1
    field[0] = jnp.zeros((CY, LANES), F32)
    field[XS + 1] = jnp.zeros((CY, LANES), F32)
    squares = jnp.zeros((CY, LANES), F32)
    for i in range(XS):
        weight = cell_weight(start, i)
        raw2 = weight * (slab_laplace(slab, edges, i) / alpha)
        raw2_out[i] = raw2
        squares = squares + raw2 * raw2
        field[i + 1] = weight * raw2
    picked = dot(r_turned[...], raw1.astype(BF16), 1, 0)
    contrib = jnp.concatenate(products_t(picked, (first, second), 0, SLOTS), axis=0)
    low, high = [], []
    for x in range(CX):
        at = tile * CX + x + 1
        f = field[at]
        beside = row_sides(f, 0.0, 0.0) + lane_sides(f) + field[at - 1] + field[at + 1]
        nq_out[CY * x : CY * x + CY, :] = 6.0 * f - beside
        low.append(f[0:1])
        high.append(f[CY - 1 : CY])
    low, high = edge_tiles(scratch, low, high, total(raw1 * raw1) + total(squares))
    send_contributions(send, p_hot[...], contrib, lambda d: jnp.where(d > ray, high, low))


def kernel_next_v(pos_ref, recv, q_ref, v0_raw, alpha0, nq, send, v_out, beta_out, scratch):
    ray = pos_ref[0]
    contrib, notes = received(recv)
    q_hot = q_ref[...]
    norm = notes[0]
    for d in range(1, RAY):
        norm = norm + notes[d]
    beta = jnp.sqrt(norm[CX : CX + 1] + (norm[CX + 1 : CX + 2] + norm[CX + 2 : CX + 3]) + eps)
    beta_out[...] = beta
    z = dot(q_hot, contrib, 0, 0)
    low = jnp.where(ray > 0, recv[jnp.maximum(ray - 1, 0)].astype(F32)[CAP:MSG], 0.0)
    high = jnp.where(ray < RAY - 1, recv[jnp.minimum(ray + 1, RAY - 1)].astype(F32)[CAP:MSG], 0.0)
    row = iota((CY, LANES), 0)
    squares = jnp.zeros((CY, LANES), F32)
    edges_low, edges_high, parts = [], [], []
    for x in range(CX):
        cut = slice(CY * x, CY * x + CY)
        edge = jnp.where(row == 0, low[x : x + 1], 0.0) + jnp.where(row == CY - 1, high[x : x + 1], 0.0)
        v_raw = (z[cut] + (nq[cut, :] - edge)) / beta - beta * (v0_raw[cut, :] / alpha0[...])
        v_out[cut, :] = v_raw
        parts.append(v_raw)
        squares = squares + v_raw * v_raw
        edges_low.append(v_raw[0:1])
        edges_high.append(v_raw[CY - 1 : CY])
    send_columns(send, q_hot, jnp.concatenate(parts, axis=0), scratch, edges_low, edges_high, total(squares), ray)


def kernel_last_norm(
    pos_ref, recv, v_raw, start, beta1, raw1_ref, raw2_ref, send, raw1_out, alpha_out, scratch, slab, edges
):
    tile = pos_ref[1]
    kv, alpha = gathered(recv, v_raw, tile, slab, edges)
    alpha_out[...] = alpha
    raw1 = kv / alpha - alpha * (raw1_ref[...] / beta1[...])
    scratch[...] = raw1.reshape(TILE, KOWN, LANES)
    rest = recv[0, TMSG : TMSG + 16, :].astype(F32)[0:KOWN]
    for t in range(1, TILE):
        rest = rest + recv[t, TMSG : TMSG + 16, :].astype(F32)[0:KOWN]
    raw1_out[...] = scratch[tile] + rest / alpha
    squares = jnp.zeros((CY, LANES), F32)
    for i in range(XS):
        raw2 = cell_weight(start, i) * (slab_laplace(slab, edges, i) / alpha) - alpha * (raw2_ref[i] / beta1[...])
        squares = squares + raw2 * raw2
    norm = total(raw1 * raw1) + total(squares)
    send[...] = jnp.broadcast_to(norm.reshape(1, 1, 1), (RAY, 1, LANES))


def kernel_end(recv, v0_raw, v1_raw, raw1, beta0, beta1, alpha0, alpha1, model_out, u_out):
    norm = recv[0]
    for d in range(1, RAY):
        norm = norm + recv[d]
    b0, b1, b2 = beta0[...], beta1[...], jnp.sqrt(norm + eps)
    a0, a1 = alpha0[...], alpha1[...]
    v0, v1 = v0_raw[...] / a0, v1_raw[...] / a1
    rho1 = jnp.sqrt(a0 * a0 + b1 * b1)
    cosine1, sine1 = a0 / rho1, b1 / rho1
    theta = sine1 * a1
    rhobar = -cosine1 * a1
    phi1, phibar = cosine1 * b0, sine1 * b0
    w1 = v1 - theta / rho1 * v0
    rho2 = jnp.sqrt(rhobar * rhobar + b2 * b2)
    phi2 = rhobar / rho2 * phibar
    model_out[...] = phi1 / rho1 * v0 + phi2 / rho2 * w1
    u_out[...] = raw1[...] / b2


VM = pl.BlockSpec(memory_space=pltpu.VMEM)
SM = pl.BlockSpec(memory_space=pltpu.SMEM)
HBM = pl.BlockSpec(memory_space=pltpu.HBM)


def call(kernel, outs, args, specs=None, scratch=(), limit=32):
    return pl.pallas_call(
        kernel,
        out_shape=[jax.ShapeDtypeStruct(shape, kind) for shape, kind in outs],
        in_specs=specs or [SM] + [VM] * (len(args) - 1),
        out_specs=[VM] * len(outs),
        scratch_shapes=[pltpu.VMEM(s, F32) if isinstance(s, tuple) else s for s in scratch],
        compiler_params=pltpu.CompilerParams(vmem_limit_bytes=limit * 2**20),
        name=getattr(kernel, "func", kernel).__name__,
    )(*args)


def shards(data, blocks, block_cols, block_rows, block_counts, reg_weight):
    pos = jnp.stack([lax.axis_index("ray"), lax.axis_index("tile")]).astype(jnp.int32)
    weight = reg_weight.reshape(CELLS, LANES)
    message = ((RAY, MSG, LANES), BF16)
    tile_message = ((TILE, TMSG, LANES), BF16)
    scalar = ((1, LANES), F32)
    cells = ((CELLS, LANES), F32)
    rays = ((KB, LANES), F32)
    slab = ((XS, CY, LANES), F32)
    edges = (2, 8, LANES)
    slabs = [(XS + 2, CY, LANES), (TILE, 8, LANES)]
    own = jnp.concatenate([data.reshape(KOWN, LANES), weight], axis=0)
    start = lax.all_to_all(jnp.broadcast_to(own, (TILE,) + own.shape), "tile", 0, 0)
    half = ((HALF, LANES, LANES), BF16)
    p_hot, p_wide, r_hot, r_turned, note, first = call(
        kernel_index,
        [
            ((RAY * CAP, SLOTS), BF16),
            ((SLOTS, RAY * MSG), BF16),
            ((KB, SLOTS), BF16),
            ((SLOTS, KB), BF16),
            ((RAY * CAP, LANES), F32),
            half,
        ],
        (block_cols[0], block_rows[0], block_counts, blocks[0, 0]),
        [VM] * 3 + [HBM],
        [pltpu.SemaphoreType.DMA((CHUNKS,))],
        50,
    )
    send, second = call(
        kernel_start,
        [message, half],
        (pos, start, note, blocks[0, 0], first, p_hot, r_turned),
        [SM, VM, VM, HBM, VM, VM, VM],
        [pltpu.SemaphoreType.DMA((CHUNKS,))],
        48,
    )
    recv = lax.all_to_all(send, "ray", 0, 0)
    send, v0_raw, q_hot, beta0 = call(
        kernel_first_v,
        [message, cells, ((RAY * CAP, CELLS), BF16), scalar],
        (pos, recv),
        scratch=[edges],
    )
    recv = lax.all_to_all(send, "ray", 0, 0)
    (send,) = call(
        functools.partial(kernel_forward, last=False), [((TILE, TMSG, LANES), BF16)],
        (pos, recv, p_wide, r_hot, first, second, v0_raw), scratch=[(16, LANES)],
    )
    recv = lax.all_to_all(send, "tile", 0, 0)
    send, raw1, raw2, alpha0, nq = call(
        kernel_back,
        [message, rays, slab, scalar, cells],
        (pos, recv, v0_raw, start, beta0, first, second, p_hot, r_turned),
        scratch=[edges] + slabs + slabs[:1],
    )
    recv = lax.all_to_all(send, "ray", 0, 0)
    send, v1_raw, beta1 = call(
        kernel_next_v,
        [((RAY, MSG, LANES), F32), cells, scalar],
        (pos, recv, q_hot, v0_raw, alpha0, nq),
        scratch=[edges],
    )
    recv = lax.all_to_all(send, "ray", 0, 0)
    (send,) = call(
        functools.partial(kernel_forward, last=True), [((TILE, TMSG + 16, LANES), BF16)],
        (pos, recv, p_wide, r_hot, first, second, v1_raw), scratch=[(16, LANES)],
    )
    recv = lax.all_to_all(send, "tile", 0, 0)
    send, raw1_own, alpha1 = call(
        kernel_last_norm,
        [((RAY, 1, LANES), F32), ((KOWN, LANES), F32), scalar],
        (pos, recv, v1_raw, start, beta1, raw1, raw2),
        scratch=[(TILE, KOWN, LANES)] + slabs,
    )
    recv = lax.all_to_all(send, "ray", 0, 0)
    model, rays = call(
        kernel_end,
        [cells, ((KOWN, LANES), F32)],
        (recv, v0_raw, v1_raw, raw1_own, beta0, beta1, alpha0, alpha1),
        [VM] * 8,
    )
    return model.reshape(reg_weight.shape), rays.reshape(data.shape)


def solution(mesh):
    return jax.shard_map(
        shards,
        mesh=mesh,
        in_specs=(
            P(("ray", "tile")),
            P("ray", "tile", None, None, None),
            P("ray", "tile", None),
            P("ray", "tile", None),
            P("ray", "tile"),
            P("tile", "ray", None),
        ),
        out_specs=(P("tile", "ray", None), P(("ray", "tile"))),
        check_vma=False,
    )
```
